32 devices in a mesh: dp: 4 (over z), cols: 8 (over y, x, core).
Axes of the slice: x: 2, y: 2, z: 4, core: 2. Of those that a mesh axis runs over, the one named last changes fastest.
Arguments:
- inputs: bfloat16 [4096, 4096], P('dp', 'cols'), may hold values from -6 to 6
- query_grads: bfloat16 [4096, 8192], P('dp'), may hold values from -0.125 to 0.125, as said below
- momentum: float32 [8192, 4096], P('dp', 'cols'), may hold values from -14 to 14, as said below
Outputs:
- new_momentum: float32 [8192, 4096], P('dp', 'cols')
- update: float32 [8192, 4096], P('dp', 'cols')
The draws below stay inside these ranges and needn't reach their ends.
Inputs may be any that keep to these rules, and one draw needn't show every extreme that they name: `query_grads`: entries of scale about 4096 ** -0.5. `momentum`: entries of order two.
All inputs are finite; a program needn't handle non-finite values.
Results may differ from the reference program's by a relative error of at most 0.0003.
Values may be sent and summed in bfloat16 or wider, within the bound.
No kernel may reach another device: no remote copies, remote signals or barrier semaphores. Data moves between devices by JAX's collectives and lax.ppermute only.
A program may use at most 128 MiB of HBM per device.

```python
import math
import jax
import jax.numpy as jnp
from jax import lax

D = 4096
HEADS = 64
HEAD_DIM = 128
NEWTON_STEPS = 5
TOKENS = 4096


def draw_query_grads(key, part):
    first = jax.random.fold_in(key, 11)
    scale = TOKENS ** (-0.5)
    shape = (TOKENS, HEADS * HEAD_DIM)
    values = jax.random.normal(first, shape, jnp.float32)
    return jnp.clip(values * scale, -8.0 * scale, 8.0 * scale).astype(jnp.bfloat16)


def draw_momentum(key, part):
    first = jax.random.fold_in(key, 21)
    shape = (HEADS * HEAD_DIM, D)
    values = 2.0 * jax.random.normal(first, shape, jnp.float32)
    return jnp.clip(values, -14.0, 14.0)


def steps_of(key, dims, split, least, top_value):
    level = 1.0
    for dim, shards_of in split:
        draws = jax.random.uniform(jax.random.fold_in(jax.random.fold_in(key, 6), dim), (shards_of,), jnp.float32, least / len(split), top_value / len(split))
        level = level * jnp.repeat(jnp.exp(draws), dims[dim] // shards_of).reshape((-1,) + (1,) * (len(dims) - 1 - dim))
    return level


def bell_draw(own_key, shape, spread, bound, shards=(), kind=jnp.bfloat16):
    drawn = spread * jax.random.normal(own_key, shape, jnp.float32)
    if shards:
        drawn = drawn * steps_of(own_key, shape, shards, -0.22, 0.18)
    return jnp.clip(drawn, -bound, bound).astype(kind)


def setup_inputs(seed: int = 0) -> dict:
    keys = jax.random.split(jax.random.key(seed), 4)
    inputs = bell_draw(keys[0], (TOKENS, D), 1.0, 6.0, ((0, 4), (1, 8)))
    query_grads = draw_query_grads(jax.random.fold_in(keys[3], 71), 0)
    momentum = draw_momentum(jax.random.fold_in(keys[3], 71), 0)
    return {"inputs": inputs, "query_grads": query_grads, "momentum": momentum}


MOMENTUM_DECAY = 0.95
NORM_EPS = 1e-07
LINEAR_COEF = 3.4445
CUBIC_COEF = -4.775
QUINTIC_COEF = 2.0315
HIGHEST = lax.Precision.HIGHEST

def polynomial(gram_matrix):
    matrix_order = gram_matrix.shape[-1]
    trace_sum = lax.optimization_barrier(jnp.sum(jnp.diagonal(gram_matrix, axis1=1, axis2=2), axis=1))
    norm_scale = jnp.sqrt(trace_sum) + NORM_EPS
    current = gram_matrix / (norm_scale * norm_scale)[:, None, None]
    identity = jnp.eye(matrix_order, dtype=jnp.float32)
    factor = jnp.broadcast_to(identity, gram_matrix.shape)
    for sweep_index in range(NEWTON_STEPS):
        square = jnp.einsum('hij,hjk->hik', current, current, precision=HIGHEST)
        poly_term = LINEAR_COEF * identity + CUBIC_COEF * current + QUINTIC_COEF * square
        factor = jnp.einsum('hij,hjk->hik', poly_term, factor, precision=HIGHEST)
        if sweep_index + 1 < NEWTON_STEPS:
            inner = jnp.einsum('hij,hjk->hik', current, poly_term, precision=HIGHEST)
            current = jnp.einsum('hij,hjk->hik', poly_term, inner, precision=HIGHEST)
    return factor / norm_scale[:, None, None]

def head_update(head_block):
    gram_matrix = jnp.dot(head_block, head_block.T, precision=HIGHEST)
    factor = polynomial(gram_matrix[None])[0]
    return math.sqrt(D) * jnp.dot(factor, head_block, precision=HIGHEST)

def reference(inputs, query_grads, momentum):
    gradient = lax.dot_general(query_grads, inputs, (((0,), (0,)), ((), ())), preferred_element_type=jnp.float32)
    new_momentum = MOMENTUM_DECAY * momentum + gradient
    blocks = new_momentum.reshape(HEADS, HEAD_DIM, D)
    update = lax.map(head_update, blocks).reshape(HEADS * HEAD_DIM, D)
    return (new_momentum, update)
```

```python
import functools
import math

import jax
import jax.numpy as jnp
from jax import lax
from jax.experimental import pallas as pl
from jax.experimental.pallas import tpu as pltpu
from jax.sharding import PartitionSpec as P

HEAD_DIM = 128
NEWTON_STEPS = 5
MOMENTUM_DECAY = 0.95
NORM_EPS = 1e-07
LINEAR_COEF = 3.4445
CUBIC_COEF = -4.775
QUINTIC_COEF = 2.0315
HIGHEST = lax.Precision.HIGHEST
CONTRACT_TOKENS = (((0,), (0,)), ((), ()))
SMALL_BYTES = 16 * 1024 * 1024
VMEM_BYTES = 32 * 1024 * 1024


def split(value):
    high = value.astype(jnp.bfloat16)
    return high, (value - high.astype(jnp.float32)).astype(jnp.bfloat16)


def dot3(left, right, dims):
    lh, ll = left
    rh, rl = right
    dot = functools.partial(lax.dot_general, dimension_numbers=dims, preferred_element_type=jnp.float32)
    return dot(lh, rh) + (dot(lh, rl) + dot(ll, rh))


def accumulate_kernel(layouts, decay, final, place, total, *refs):
    refs = list(refs)
    taken = [([refs.pop(0) for _ in layout], layout, refs.pop(0)) for layout in layouts]
    out = refs.pop(0)
    out[...] = total[...] * decay if decay else total[...]
    pair_rows = out.shape[0] // 2
    for q_refs, layout, x_ref in taken:
        for q_ref, piece in zip(q_refs, layout):
            if piece is None:
                out[...] += lax.dot_general(
                    q_ref[...], x_ref[...], CONTRACT_TOKENS, preferred_element_type=jnp.float32
                )
                continue
            core, offset, count = piece
            start = pl.multiple_of(((place[1] + core) % 2) * pair_rows + offset, count)
            value = jnp.dot(q_ref[0], x_ref[...], preferred_element_type=jnp.float32)
            out[pl.ds(start, count), :] += value
    if not final:
        return
    gram = refs.pop(0)
    pair_heads = gram.shape[1]
    for head in range(out.shape[0] // HEAD_DIM):
        parts = split(out[head * HEAD_DIM : (head + 1) * HEAD_DIM, :])
        pair = pl.program_id(0) * 2 + head // pair_heads
        other = place[1] ^ pair
        slot = other // 2 + (other % 2) * (gram.shape[0] // 2)
        gram[slot, head % pair_heads] = dot3(parts, parts, (((1,), (1,)), ((), ())))


def polynomial_kernel(*refs):
    parts, factor = refs[:-1], refs[-1]
    gram = functools.reduce(lambda total, piece: total + piece[...], parts[1:], parts[0][...])
    order = gram.shape[-1]
    rows = lax.broadcasted_iota(jnp.int32, (order, order), 0)
    cols = lax.broadcasted_iota(jnp.int32, (order, order), 1)
    identity = (rows == cols).astype(jnp.float32)
    heads = range(gram.shape[0])
    dot = functools.partial(jnp.dot, precision=HIGHEST, preferred_element_type=jnp.float32)
    norms = [jnp.sqrt(jnp.sum(gram[h] * identity)) + NORM_EPS for h in heads]
    current = [gram[h] / (norms[h] * norms[h]) for h in heads]
    factors = [None for h in heads]
    for sweep in range(NEWTON_STEPS):
        square = [dot(current[h], current[h]) for h in heads]
        poly = [LINEAR_COEF * identity + CUBIC_COEF * current[h] + QUINTIC_COEF * square[h] for h in heads]
        factors = [poly[h] if sweep == 0 else dot(poly[h], factors[h]) for h in heads]
        if sweep + 1 < NEWTON_STEPS:
            inner = [dot(current[h], poly[h]) for h in heads]
            current = [dot(poly[h], inner[h]) for h in heads]
    for h in heads:
        factor[h] = factors[h] / norms[h]


def update_kernel(scale, place, factor, block, *refs):
    update = refs[-1]
    for head in range(factor.shape[1]):
        rows = slice(head * HEAD_DIM, (head + 1) * HEAD_DIM)
        product = dot3(split(factor[0, head]), split(block[rows, :]), (((1,), (0,)), ((), ())))
        update[rows, :] = scale * product


def shards(model_width, inputs, query_grads, momentum):
    depth = lax.axis_size("dp")
    owners = lax.axis_size("cols")
    z = lax.axis_index("dp")
    c = lax.axis_index("cols")
    tokens, col_count = inputs.shape
    row_count = momentum.shape[0]
    pair_rows = row_count // owners
    pair_heads = pair_rows // HEAD_DIM
    def over(bits, value):
        return lax.ppermute(value, "cols", [(i, i ^ bits) for i in range(owners)])

    def onward(k, value):
        return lax.ppermute(value, "dp", [(i, (i + k) % depth) for i in range(depth)])

    def both(held, got):
        return [jnp.concatenate(pair) for pair in zip(held, got)]

    pieces = [
        lax.dynamic_slice(query_grads, (0, lax.rem(z + k, depth) * row_count + c * pair_rows), (tokens, pair_rows)).T
        for k in range(1, depth)
    ]
    turns = ((4, 2), (2, 4))
    half = pair_rows // 2

    near = [onward(k, pieces[k - 1]) for k in (1, 3)]
    near, pieces = lax.optimization_barrier((near, pieces))

    far = onward(2, pieces[1])
    near = [piece[None] for piece in near]
    got = [over(turn[0], piece) for turn, piece in zip(turns, near)]
    far, near, got, moved = lax.optimization_barrier((far, near, got, inputs))

    moved_1 = onward(1, moved)
    near = both(near, got)
    got = [over(turn[1], piece) for turn, piece in zip(turns, near)]
    far, near, got, moved_1 = lax.optimization_barrier((far, near, got, moved_1))

    moved_2 = onward(1, moved_1)
    near = both(near, got)
    near_got = [over(1, piece) for piece in near]
    far = [far[None, :half], far[None, half:]]
    far = both(far, [over(turn[0], piece) for turn, piece in zip(turns, far)])
    got = [over(turn[1], piece) for turn, piece in zip(turns, far)]
    far, near, near_got, got, moved_1, moved_2 = lax.optimization_barrier((far, near, near_got, got, moved_1, moved_2))

    moved_3 = onward(1, moved_2)
    far = both(far, got)
    far_got = [over(1, piece) for piece in far]

    place = jnp.stack([z, c]).astype(jnp.int32)

    def pair_of(i, place):
        return place[1] ^ ((i % 4) * 2 + i // 4)

    def rows_spec(part, columns):
        return pl.BlockSpec((pair_rows, columns), lambda i, place: (pair_of(i, place), part))

    pairs = 2
    gram_dims = (owners, pair_heads, HEAD_DIM, HEAD_DIM)
    gram_spec = pl.BlockSpec(gram_dims, lambda i, place: (0, 0, 0, 0))
    gram_shape = jax.ShapeDtypeStruct(gram_dims, jnp.float32)

    def spots(order):
        def index_map(i, place):
            other = (place[1] // 2) ^ i
            return (other if order else (other % 2) * 2 + other // 2), 0, 0

        return index_map

    def term_specs(layout):
        if layout[0] is None:
            return [pl.BlockSpec((tokens, pairs * pair_rows), lambda i, place: (0, place[0] * (owners // pairs) + i))]
        return [pl.BlockSpec((1, count, tokens), spots(order)) for _, _, count, order in layout]

    def accumulate(total, terms, decay, final):
        block = pl.BlockSpec((pairs * pair_rows, col_count), lambda i, place: (i, 0))
        whole = pl.BlockSpec((tokens, col_count), lambda i, place: (0, 0))
        arrays = [array for rows, _, x in terms for array in (*rows, x)]
        shape = jax.ShapeDtypeStruct((row_count, col_count), jnp.float32)
        layouts = [[piece and piece[:3] for piece in layout] for _, layout, _ in terms]
        return pl.pallas_call(
            functools.partial(accumulate_kernel, layouts, decay, final),
            grid_spec=pltpu.PrefetchScalarGridSpec(
                num_scalar_prefetch=1,
                grid=(owners // pairs,),
                in_specs=[block] + [spec for _, layout, _ in terms for spec in (*term_specs(layout), whole)],
                out_specs=[block, gram_spec] if final else block,
            ),
            out_shape=[shape, gram_shape] if final else shape,
            compiler_params=pltpu.CompilerParams(vmem_limit_bytes=VMEM_BYTES),
            cost_estimate=pl.CostEstimate(
                flops=2 * len(terms) * tokens * row_count * col_count,
                bytes_accessed=2 * row_count * (len(terms) * tokens + 4 * col_count),
                transcendentals=0,
            ),
        )(place, total, *arrays)

    whole_pair = [[(core, 0, pair_rows, order) for core in range(2)] for order in range(2)]
    halves = [(core, part * half, half, part) for part in range(2) for core in range(2)]
    own = ([query_grads], [None], inputs)
    one = ([near[0], near_got[0]], whole_pair[0], moved_1)
    two = ([far[0], far_got[0], far[1], far_got[1]], halves, moved_2)
    three = ([near[1], near_got[1]], whole_pair[1], moved_3)
    total = accumulate(momentum, [own, one], MOMENTUM_DECAY, False)
    total = accumulate(total, [two], None, False)
    new_momentum, gram = accumulate(total, [three], None, True)

    four = gram[:4] + over(1, gram[4:])
    pieces = [four[0]] + [over(2 * i, four[i]) for i in range(1, 4)]
    factor = pl.pallas_call(
        polynomial_kernel,
        out_shape=jax.ShapeDtypeStruct(pieces[0].shape, jnp.float32),
        compiler_params=pltpu.CompilerParams(vmem_limit_bytes=SMALL_BYTES),
    )(*pieces)
    factors = jnp.stack([factor] + [over(2 * i, factor) for i in range(1, 4)])
    others = over(1, factors)

    def update_half(core, values, *before):
        def spec():
            return pl.BlockSpec((pair_rows, col_count), lambda i, place: (pair_of(i + core * (owners // 2), place), 0))

        return pl.pallas_call(
            functools.partial(update_kernel, math.sqrt(model_width)),
            grid_spec=pltpu.PrefetchScalarGridSpec(
                num_scalar_prefetch=1,
                grid=(owners // 2,),
                in_specs=[
                    pl.BlockSpec((1, pair_heads, HEAD_DIM, HEAD_DIM), lambda i, place: (i, 0, 0, 0)),
                    spec(),
                ]
                + [pl.BlockSpec(memory_space=pl.ANY)] * len(before),
                out_specs=spec(),
            ),
            out_shape=jax.ShapeDtypeStruct((row_count, col_count), jnp.float32),
            input_output_aliases={3: 0} if before else {},
            compiler_params=pltpu.CompilerParams(vmem_limit_bytes=SMALL_BYTES),
            cost_estimate=pl.CostEstimate(
                flops=3 * row_count * col_count * HEAD_DIM, bytes_accessed=4 * row_count * col_count, transcendentals=0
            ),
        )(place, values, new_momentum, *before)

    return new_momentum, update_half(1, others, update_half(0, factors))


def polynomial(gram_matrix):
    matrix_order = gram_matrix.shape[-1]
    trace_sum = jnp.sum(jnp.diagonal(gram_matrix, axis1=1, axis2=2), axis=1)
    norm_scale = jnp.sqrt(trace_sum) + NORM_EPS
    current = gram_matrix / (norm_scale * norm_scale)[:, None, None]
    identity = jnp.eye(matrix_order, dtype=jnp.float32)
    factor = jnp.broadcast_to(identity, gram_matrix.shape)
    for sweep_index in range(NEWTON_STEPS):
        square = jnp.einsum("hij,hjk->hik", current, current, precision=HIGHEST)
        poly_term = LINEAR_COEF * identity + CUBIC_COEF * current + QUINTIC_COEF * square
        factor = jnp.einsum("hij,hjk->hik", poly_term, factor, precision=HIGHEST)
        if sweep_index + 1 < NEWTON_STEPS:
            inner = jnp.einsum("hij,hjk->hik", current, poly_term, precision=HIGHEST)
            current = jnp.einsum("hij,hjk->hik", poly_term, inner, precision=HIGHEST)
    return factor / norm_scale[:, None, None]


def plain_shards(model_width, inputs, query_grads, momentum):
    row_count, col_count = momentum.shape
    gradient = lax.psum_scatter(
        lax.dot_general(query_grads, inputs, CONTRACT_TOKENS, preferred_element_type=jnp.float32),
        "dp",
        scatter_dimension=0,
        tiled=True,
    )
    new_momentum = MOMENTUM_DECAY * momentum + gradient
    local_heads = row_count // HEAD_DIM
    blocks = new_momentum.reshape(local_heads, HEAD_DIM, col_count)
    partial_value = jnp.einsum("hik,hjk->hij", blocks, blocks, precision=HIGHEST)
    owners = lax.axis_size("cols")
    slot_count = -(-local_heads // owners)
    padded = jnp.pad(partial_value, ((0, slot_count * owners - local_heads), (0, 0), (0, 0)))
    owned_gram = lax.psum_scatter(
        padded.reshape(slot_count, owners, HEAD_DIM, HEAD_DIM), "cols", scatter_dimension=1, tiled=True
    )
    owned_factor = polynomial(owned_gram.reshape(slot_count, HEAD_DIM, HEAD_DIM))
    returned = lax.all_gather(
        owned_factor.reshape(slot_count, 1, HEAD_DIM, HEAD_DIM), "cols", axis=1, tiled=True
    )
    factor = returned.reshape(slot_count * owners, HEAD_DIM, HEAD_DIM)[:local_heads]
    update = math.sqrt(model_width) * jnp.einsum("hij,hjk->hik", factor, blocks, precision=HIGHEST)
    return new_momentum, update.reshape(row_count, col_count)


def solution(mesh):
    depth, owners = mesh.shape["dp"], mesh.shape["cols"]

    def run(inputs, query_grads, momentum):
        local_heads = momentum.shape[0] // depth // HEAD_DIM
        chosen = shards if (depth, owners) == (4, 8) and local_heads % owners == 0 else plain_shards
        return jax.shard_map(
            functools.partial(chosen, momentum.shape[1]),
            mesh=mesh,
            in_specs=(P("dp", "cols"), P("dp", None), P("dp", "cols")),
            out_specs=(P("dp", "cols"), P("dp", "cols")),
            check_vma=False,
        )(inputs, query_grads, momentum)

    return run
```

```python
import functools
import math

import jax
import jax.numpy as jnp
from jax import lax
from jax.experimental import pallas as pl
from jax.experimental.pallas import tpu as pltpu
from jax.sharding import PartitionSpec as P

HEAD_DIM = 128
NEWTON_STEPS = 5
MOMENTUM_DECAY = 0.95
NORM_EPS = 1e-07
LINEAR_COEF = 3.4445
CUBIC_COEF = -4.775
QUINTIC_COEF = 2.0315
HIGHEST = lax.Precision.HIGHEST
CONTRACT_TOKENS = (((0,), (0,)), ((), ()))
SMALL_BYTES = 16 * 1024 * 1024
VMEM_BYTES = 32 * 1024 * 1024


def split(value):
    high = value.astype(jnp.bfloat16)
    return high, (value - high.astype(jnp.float32)).astype(jnp.bfloat16)


def dot3(left, right, dims):
    lh, ll = left
    rh, rl = right
    dot = functools.partial(lax.dot_general, dimension_numbers=dims, preferred_element_type=jnp.float32)
    return dot(lh, rh) + (dot(lh, rl) + dot(ll, rh))


def accumulate_kernel(layouts, decay, place, total, *refs):
    refs, out = list(refs[:-1]), refs[-1]
    out[...] = total[...] * decay if decay else total[...]
    pair_rows = out.shape[0] // 2
    for layout in layouts:
        q_refs, x_ref = [refs.pop(0) for _ in layout], refs.pop(0)
        for q_ref, piece in zip(q_refs, layout):
            if piece is None:
                out[...] += lax.dot_general(
                    q_ref[...], x_ref[...], CONTRACT_TOKENS, preferred_element_type=jnp.float32
                )
                continue
            core, offset, count = piece
            start = pl.multiple_of(((place[1] + core) % 2) * pair_rows + offset, count)
            value = jnp.dot(q_ref[0], x_ref[...], preferred_element_type=jnp.float32)
            out[pl.ds(start, count), :] += value


def rows_at(place, core, index, count):
    return pl.ds(pl.multiple_of((place[1] ^ (2 * index + core)) * count, count), count)


def last_kernel(core, place, total, queries, x_ref, *refs):
    new_momentum, blocks, gram, sems = refs[-4:]
    copies = []
    count = queries.shape[1]
    depth = queries.shape[2]
    product = jnp.dot(queries[...].reshape(-1, depth), x_ref[...], preferred_element_type=jnp.float32)
    for index in range(queries.shape[0]):
        rows = rows_at(place, core, index, count)
        value = total[rows, :] + product[index * count : (index + 1) * count, :]
        blocks[index] = value
        copies.append(pltpu.make_async_copy(blocks.at[index], new_momentum.at[rows, :], sems.at[index]))
        copies[-1].start()
        for head in range(gram.shape[1]):
            parts = split(value[head * HEAD_DIM : (head + 1) * HEAD_DIM, :])
            gram[index, head] = dot3(parts, parts, (((1,), (1,)), ((), ())))
    for copy in copies:
        copy.wait()


def polynomial_kernel(*refs):
    parts, factor = refs[:-1], refs[-1]
    gram = functools.reduce(lambda total, piece: total + piece[...], parts[1:], parts[0][...])
    order = gram.shape[-1]
    rows = lax.broadcasted_iota(jnp.int32, (order, order), 0)
    cols = lax.broadcasted_iota(jnp.int32, (order, order), 1)
    identity = (rows == cols).astype(jnp.float32)
    heads = range(gram.shape[0])

    def dot(left, right):
        return dot3(split(left), split(right), (((1,), (0,)), ((), ())))

    norms = [jnp.sqrt(jnp.sum(gram[h] * identity)) + NORM_EPS for h in heads]
    current = [gram[h] / (norms[h] * norms[h]) for h in heads]
    factors = [None for h in heads]
    for sweep in range(NEWTON_STEPS):
        square = [dot(current[h], current[h]) for h in heads]
        poly = [LINEAR_COEF * identity + CUBIC_COEF * current[h] + QUINTIC_COEF * square[h] for h in heads]
        factors = [poly[h] if sweep == 0 else dot(poly[h], factors[h]) for h in heads]
        if sweep + 1 < NEWTON_STEPS:
            inner = [dot(current[h], poly[h]) for h in heads]
            current = [dot(poly[h], inner[h]) for h in heads]
    for h in heads:
        factor[h] = factors[h] / norms[h]


def update_kernel(scale, core, place, factor, blocks, *refs):
    update, held, sems = refs[-3:]
    copies = []
    for index in range(blocks.shape[0]):
        for head in range(factor.shape[1]):
            rows = slice(head * HEAD_DIM, (head + 1) * HEAD_DIM)
            product = dot3(split(factor[index, head]), split(blocks[index, rows, :]), (((1,), (0,)), ((), ())))
            held[index, rows, :] = scale * product
        rows = rows_at(place, core, index, blocks.shape[1])
        copies.append(pltpu.make_async_copy(held.at[index], update.at[rows, :], sems.at[index]))
        copies[-1].start()
    for copy in copies:
        copy.wait()


def shards(model_width, inputs, query_grads, momentum):
    depth = lax.axis_size("dp")
    owners = lax.axis_size("cols")
    z = lax.axis_index("dp")
    c = lax.axis_index("cols")
    tokens, col_count = inputs.shape
    row_count = momentum.shape[0]
    pair_rows = row_count // owners
    pair_heads = pair_rows // HEAD_DIM
    def over(bits, value):
        return lax.ppermute(value, "cols", [(i, i ^ bits) for i in range(owners)])

    def onward(k, value):
        return lax.ppermute(value, "dp", [(i, (i + k) % depth) for i in range(depth)])

    def both(held, got):
        return [jnp.concatenate(pair) for pair in zip(held, got)]

    pieces = [
        lax.dynamic_slice(query_grads, (0, lax.rem(z + k, depth) * row_count + c * pair_rows), (tokens, pair_rows)).T
        for k in range(1, depth)
    ]
    turns = ((4, 2), (2, 4))
    half = pair_rows // 2

    near = [onward(k, pieces[k - 1]) for k in (1, 3)]
    near, pieces = lax.optimization_barrier((near, pieces))

    far = onward(2, pieces[1])
    near = [piece[None] for piece in near]
    got = [over(turn[0], piece) for turn, piece in zip(turns, near)]
    far, near, got, moved = lax.optimization_barrier((far, near, got, inputs))

    moved_1 = onward(1, moved)
    near = both(near, got)
    got = [over(turn[1], piece) for turn, piece in zip(turns, near)]
    far, near, got, moved_1 = lax.optimization_barrier((far, near, got, moved_1))

    moved_2 = onward(1, moved_1)
    near = both(near, got)
    near_got = [over(1, piece) for piece in near]
    far = [far[None, :half], far[None, half:]]
    far = both(far, [over(turn[0], piece) for turn, piece in zip(turns, far)])
    got = [over(turn[1], piece) for turn, piece in zip(turns, far)]
    far, near, near_got, got, moved_1, moved_2 = lax.optimization_barrier((far, near, near_got, got, moved_1, moved_2))

    moved_3 = onward(1, moved_2)
    far = both(far, got)
    far_got = [over(1, piece) for piece in far]

    place = jnp.stack([z, c]).astype(jnp.int32)

    def pair_of(i, place):
        return place[1] ^ ((i % 4) * 2 + i // 4)

    def rows_spec(part, columns):
        return pl.BlockSpec((pair_rows, columns), lambda i, place: (pair_of(i, place), part))

    pairs = 2
    def spots(order):
        def index_map(i, place):
            other = (place[1] // 2) ^ i
            return (other if order else (other % 2) * 2 + other // 2), 0, 0

        return index_map

    def term_specs(layout):
        if layout[0] is None:
            return [pl.BlockSpec((tokens, pairs * pair_rows), lambda i, place: (0, place[0] * (owners // pairs) + i))]
        return [pl.BlockSpec((1, count, tokens), spots(order)) for _, _, count, order in layout]

    def accumulate(total, terms, decay):
        block = pl.BlockSpec((pairs * pair_rows, col_count), lambda i, place: (i, 0))
        whole = pl.BlockSpec((tokens, col_count), lambda i, place: (0, 0))
        arrays = [array for rows, _, x in terms for array in (*rows, x)]
        shape = jax.ShapeDtypeStruct((row_count, col_count), jnp.float32)
        layouts = [[piece and piece[:3] for piece in layout] for _, layout, _ in terms]
        return pl.pallas_call(
            functools.partial(accumulate_kernel, layouts, decay),
            grid_spec=pltpu.PrefetchScalarGridSpec(
                num_scalar_prefetch=1,
                grid=(owners // pairs,),
                in_specs=[block] + [spec for _, layout, _ in terms for spec in (*term_specs(layout), whole)],
                out_specs=block,
            ),
            out_shape=shape,
            compiler_params=pltpu.CompilerParams(vmem_limit_bytes=VMEM_BYTES),
            cost_estimate=pl.CostEstimate(
                flops=2 * len(terms) * tokens * row_count * col_count,
                bytes_accessed=2 * row_count * (len(terms) * tokens + 4 * col_count),
                transcendentals=0,
            ),
        )(place, total, *arrays)

    whole_pair = [[(core, 0, pair_rows, order) for core in range(2)] for order in range(2)]
    halves = [(core, part * half, half, part) for part in range(2) for core in range(2)]
    own = ([query_grads], [None], inputs)
    one = ([near[0], near_got[0]], whole_pair[0], moved_1)
    two = ([far[0], far_got[0], far[1], far_got[1]], halves, moved_2)
    total = accumulate(momentum, [own, one], MOMENTUM_DECAY)
    total = accumulate(total, [two], None)

    whole_vmem = pl.BlockSpec(memory_space=pltpu.VMEM)
    anywhere = pl.BlockSpec(memory_space=pl.ANY)
    in_smem = pl.BlockSpec(memory_space=pltpu.SMEM)
    count = owners // 2
    whole_shape = jax.ShapeDtypeStruct((row_count, col_count), jnp.float32)
    block_shape = jax.ShapeDtypeStruct((count, pair_rows, col_count), jnp.float32)

    def last(core, rows, *before):
        return pl.pallas_call(
            functools.partial(last_kernel, core),
            in_specs=[in_smem] + [whole_vmem] * 3 + [anywhere] * len(before),
            out_specs=[anywhere, whole_vmem, whole_vmem],
            out_shape=[
                whole_shape,
                block_shape,
                jax.ShapeDtypeStruct((count, pair_heads, HEAD_DIM, HEAD_DIM), jnp.float32),
            ],
            scratch_shapes=[pltpu.SemaphoreType.DMA((count,))],
            input_output_aliases={4: 0} if before else {},
            compiler_params=pltpu.CompilerParams(vmem_limit_bytes=VMEM_BYTES),
            cost_estimate=pl.CostEstimate(
                flops=tokens * row_count * col_count, bytes_accessed=2 * row_count * col_count, transcendentals=0
            ),
        )(place, total, rows, moved_3, *before)

    new_momentum, other_blocks, gram = last(1, near_got[1])
    arrived = over(1, gram)
    new_momentum, own_blocks, gram = last(0, near[1], new_momentum)
    four = gram + arrived
    pieces = [four[0]] + [over(2 * i, four[i]) for i in range(1, 4)]
    factor = pl.pallas_call(
        polynomial_kernel,
        out_shape=jax.ShapeDtypeStruct(pieces[0].shape, jnp.float32),
        compiler_params=pltpu.CompilerParams(vmem_limit_bytes=SMALL_BYTES),
    )(*pieces)
    factors = jnp.stack([factor] + [over(2 * i, factor) for i in range(1, 4)])
    others = over(1, factors)

    def update_half(core, values, blocks, *before):
        return pl.pallas_call(
            functools.partial(update_kernel, math.sqrt(model_width), core),
            in_specs=[in_smem] + [whole_vmem] * 2 + [anywhere] * len(before),
            out_specs=anywhere,
            out_shape=whole_shape,
            scratch_shapes=[pltpu.VMEM(blocks.shape, jnp.float32), pltpu.SemaphoreType.DMA((count,))],
            input_output_aliases={3: 0} if before else {},
            compiler_params=pltpu.CompilerParams(vmem_limit_bytes=SMALL_BYTES),
            cost_estimate=pl.CostEstimate(
                flops=3 * row_count * col_count * HEAD_DIM, bytes_accessed=4 * row_count * col_count, transcendentals=0
            ),
        )(place, values, blocks, *before)

    return new_momentum, update_half(1, others, other_blocks, update_half(0, factors, own_blocks))


def polynomial(gram_matrix):
    matrix_order = gram_matrix.shape[-1]
    trace_sum = jnp.sum(jnp.diagonal(gram_matrix, axis1=1, axis2=2), axis=1)
    norm_scale = jnp.sqrt(trace_sum) + NORM_EPS
    current = gram_matrix / (norm_scale * norm_scale)[:, None, None]
    identity = jnp.eye(matrix_order, dtype=jnp.float32)
    factor = jnp.broadcast_to(identity, gram_matrix.shape)
    for sweep_index in range(NEWTON_STEPS):
        square = jnp.einsum("hij,hjk->hik", current, current, precision=HIGHEST)
        poly_term = LINEAR_COEF * identity + CUBIC_COEF * current + QUINTIC_COEF * square
        factor = jnp.einsum("hij,hjk->hik", poly_term, factor, precision=HIGHEST)
        if sweep_index + 1 < NEWTON_STEPS:
            inner = jnp.einsum("hij,hjk->hik", current, poly_term, precision=HIGHEST)
            current = jnp.einsum("hij,hjk->hik", poly_term, inner, precision=HIGHEST)
    return factor / norm_scale[:, None, None]


def plain_shards(model_width, inputs, query_grads, momentum):
    row_count, col_count = momentum.shape
    gradient = lax.psum_scatter(
        lax.dot_general(query_grads, inputs, CONTRACT_TOKENS, preferred_element_type=jnp.float32),
        "dp",
        scatter_dimension=0,
        tiled=True,
    )
    new_momentum = MOMENTUM_DECAY * momentum + gradient
    local_heads = row_count // HEAD_DIM
    blocks = new_momentum.reshape(local_heads, HEAD_DIM, col_count)
    partial_value = jnp.einsum("hik,hjk->hij", blocks, blocks, precision=HIGHEST)
    owners = lax.axis_size("cols")
    slot_count = -(-local_heads // owners)
    padded = jnp.pad(partial_value, ((0, slot_count * owners - local_heads), (0, 0), (0, 0)))
    owned_gram = lax.psum_scatter(
        padded.reshape(slot_count, owners, HEAD_DIM, HEAD_DIM), "cols", scatter_dimension=1, tiled=True
    )
    owned_factor = polynomial(owned_gram.reshape(slot_count, HEAD_DIM, HEAD_DIM))
    returned = lax.all_gather(
        owned_factor.reshape(slot_count, 1, HEAD_DIM, HEAD_DIM), "cols", axis=1, tiled=True
    )
    factor = returned.reshape(slot_count * owners, HEAD_DIM, HEAD_DIM)[:local_heads]
    update = math.sqrt(model_width) * jnp.einsum("hij,hjk->hik", factor, blocks, precision=HIGHEST)
    return new_momentum, update.reshape(row_count, col_count)


def solution(mesh):
    depth, owners = mesh.shape["dp"], mesh.shape["cols"]

    def run(inputs, query_grads, momentum):
        local_heads = momentum.shape[0] // depth // HEAD_DIM
        chosen = shards if (depth, owners) == (4, 8) and local_heads % owners == 0 else plain_shards
        return jax.shard_map(
            functools.partial(chosen, momentum.shape[1]),
            mesh=mesh,
            in_specs=(P("dp", "cols"), P("dp", None), P("dp", "cols")),
            out_specs=(P("dp", "cols"), P("dp", "cols")),
            check_vma=False,
        )(inputs, query_grads, momentum)

    return run
```

```python
import functools
import math

import jax
import jax.numpy as jnp
from jax import lax
from jax.experimental import pallas as pl
from jax.experimental.pallas import tpu as pltpu
from jax.sharding import PartitionSpec as P

HEAD_DIM = 128
NEWTON_STEPS = 5
MOMENTUM_DECAY = 0.95
NORM_EPS = 1e-07
LINEAR_COEF = 3.4445
CUBIC_COEF = -4.775
QUINTIC_COEF = 2.0315
HIGHEST = lax.Precision.HIGHEST
CONTRACT_TOKENS = (((0,), (0,)), ((), ()))
SMALL_BYTES = 16 * 1024 * 1024
VMEM_BYTES = 32 * 1024 * 1024


def split(value):
    high = value.astype(jnp.bfloat16)
    return high, (value - high.astype(jnp.float32)).astype(jnp.bfloat16)


def dot3(left, right):
    dot = functools.partial(jnp.dot, preferred_element_type=jnp.float32)
    both = dot(jnp.concatenate(left), right[0])
    rows = left[0].shape[0]
    return both[:rows] + (both[rows:] + dot(left[0], right[1]))


def gram_of(block):
    high, low = split(block)
    both = lax.dot_general(
        jnp.concatenate([high, low]), high, (((1,), (1,)), ((), ())), preferred_element_type=jnp.float32
    )
    rows = high.shape[0]
    cross = both[rows:]
    return both[:rows] + (cross + cross.T)


def accumulate_kernel(layouts, decay, place, total, *refs):
    refs, out = list(refs[:-1]), refs[-1]
    out[...] = total[...] * decay if decay else total[...]
    pair_rows = out.shape[0] // 2
    for layout in layouts:
        q_refs, x_ref = [refs.pop(0) for _ in layout], refs.pop(0)
        for q_ref, piece in zip(q_refs, layout):
            if piece is None:
                out[...] += lax.dot_general(
                    q_ref[...], x_ref[...], CONTRACT_TOKENS, preferred_element_type=jnp.float32
                )
                continue
            core, offset, count = piece
            start = pl.multiple_of(((place[1] + core) % 2) * pair_rows + offset, count)
            value = jnp.dot(q_ref[0], x_ref[...], preferred_element_type=jnp.float32)
            out[pl.ds(start, count), :] += value


def rows_at(place, core, index, count):
    return pl.ds(pl.multiple_of((place[1] ^ (2 * index + core)) * count, count), count)


def last_kernel(core, place, total, queries, x_ref, blocks, gram):
    count = queries.shape[1]
    depth = queries.shape[2]
    product = jnp.dot(queries[...].reshape(-1, depth), x_ref[...], preferred_element_type=jnp.float32)
    for index in range(queries.shape[0]):
        value = total[rows_at(place, core, index, count), :] + product[index * count : (index + 1) * count, :]
        blocks[index] = value
        for head in range(gram.shape[1]):
            gram[index, head] = gram_of(value[head * HEAD_DIM : (head + 1) * HEAD_DIM, :])


def store_kernel(place, own, other, out, sems):
    copies = []
    for core, blocks in enumerate((own, other)):
        for index in range(blocks.shape[0]):
            rows = rows_at(place, core, index, blocks.shape[1])
            copies.append(pltpu.make_async_copy(blocks.at[index], out.at[rows, :], sems.at[core, index]))
            copies[-1].start()
    for copy in copies:
        copy.wait()


def polynomial_kernel(*refs):
    parts, factor = refs[:-1], refs[-1]
    gram = functools.reduce(lambda total, piece: total + piece[...], parts[1:], parts[0][...])
    order = gram.shape[-1]
    rows = lax.broadcasted_iota(jnp.int32, (order, order), 0)
    cols = lax.broadcasted_iota(jnp.int32, (order, order), 1)
    identity = (rows == cols).astype(jnp.float32)
    heads = range(gram.shape[0])

    dot = functools.partial(jnp.dot, precision=HIGHEST, preferred_element_type=jnp.float32)
    norms = [jnp.sqrt(jnp.sum(gram[h] * identity)) + NORM_EPS for h in heads]
    current = [gram[h] / (norms[h] * norms[h]) for h in heads]
    factors = [None for h in heads]
    for sweep in range(NEWTON_STEPS):
        square = [dot(current[h], current[h]) for h in heads]
        poly = [LINEAR_COEF * identity + CUBIC_COEF * current[h] + QUINTIC_COEF * square[h] for h in heads]
        factors = [poly[h] if sweep == 0 else dot(poly[h], factors[h]) for h in heads]
        if sweep + 1 < NEWTON_STEPS:
            inner = [dot(current[h], poly[h]) for h in heads]
            current = [dot(poly[h], inner[h]) for h in heads]
    for h in heads:
        factor[h] = factors[h] / norms[h]


def updated(scale, factor, block):
    heads = []
    for head in range(factor.shape[0]):
        rows = slice(head * HEAD_DIM, (head + 1) * HEAD_DIM)
        heads.append(scale * dot3(split(factor[head]), split(block[rows, :])))
    return jnp.concatenate(heads)


def own_update_kernel(scale, factor, blocks, held):
    for index in range(blocks.shape[0]):
        held[index] = updated(scale, factor[index], blocks[index])


def other_update_kernel(scale, place, factor, blocks, own, update, held, sems):
    def send(core, source, index):
        rows = rows_at(place, core, index, blocks.shape[1])
        copy = pltpu.make_async_copy(source.at[index], update.at[rows, :], sems.at[core, index])
        copy.start()
        return copy

    copies = [send(0, own, index) for index in range(own.shape[0])]
    for index in range(blocks.shape[0]):
        held[index] = updated(scale, factor[index], blocks[index])
        copies.append(send(1, held, index))
    for copy in copies:
        copy.wait()


def shards(model_width, inputs, query_grads, momentum):
    depth = lax.axis_size("dp")
    owners = lax.axis_size("cols")
    z = lax.axis_index("dp")
    c = lax.axis_index("cols")
    tokens, col_count = inputs.shape
    row_count = momentum.shape[0]
    pair_rows = row_count // owners
    pair_heads = pair_rows // HEAD_DIM
    def over(bits, value):
        return lax.ppermute(value, "cols", [(i, i ^ bits) for i in range(owners)])

    def onward(k, value):
        return lax.ppermute(value, "dp", [(i, (i + k) % depth) for i in range(depth)])

    def over_halves(bits, value):
        axis = 0 if value.shape[0] > 1 else 1
        return jnp.concatenate([over(bits, piece) for piece in jnp.split(value, 2, axis)], axis)

    def both(held, got):
        return [jnp.concatenate(pair) for pair in zip(held, got)]

    pieces = [
        lax.dynamic_slice(query_grads, (0, lax.rem(z + k, depth) * row_count + c * pair_rows), (tokens, pair_rows)).T
        for k in range(1, depth)
    ]
    turns = ((4, 2), (2, 4))
    half = pair_rows // 2

    near = [onward(k, pieces[k - 1]) for k in (1, 3)]
    near, pieces = lax.optimization_barrier((near, pieces))

    far = onward(2, pieces[1])
    near = [piece[None] for piece in near]
    got = [over_halves(turn[0], piece) for turn, piece in zip(turns, near)]
    far, near, got, moved = lax.optimization_barrier((far, near, got, inputs))

    moved_1 = onward(1, moved)
    near = both(near, got)
    got = [over_halves(turn[1], piece) for turn, piece in zip(turns, near)]
    far, near, got, moved_1 = lax.optimization_barrier((far, near, got, moved_1))

    moved_2 = onward(1, moved_1)
    near = both(near, got)
    near_got = [over(1, piece) for piece in near]
    far = [far[None, :half], far[None, half:]]
    far = both(far, [over(turn[0], piece) for turn, piece in zip(turns, far)])
    got = [over(turn[1], piece) for turn, piece in zip(turns, far)]
    far, near, near_got, got, moved_1, moved_2 = lax.optimization_barrier((far, near, near_got, got, moved_1, moved_2))

    moved_3 = onward(1, moved_2)
    far = both(far, got)
    far_got = [over(1, piece) for piece in far]

    place = jnp.stack([z, c]).astype(jnp.int32)

    def pair_of(i, place):
        return place[1] ^ ((i % 4) * 2 + i // 4)

    def rows_spec(part, columns):
        return pl.BlockSpec((pair_rows, columns), lambda i, place: (pair_of(i, place), part))

    pairs = 2
    def spots(order):
        def index_map(i, place):
            other = (place[1] // 2) ^ i
            return (other if order else (other % 2) * 2 + other // 2), 0, 0

        return index_map

    def term_specs(layout):
        if layout[0] is None:
            return [pl.BlockSpec((tokens, pairs * pair_rows), lambda i, place: (0, place[0] * (owners // pairs) + i))]
        return [pl.BlockSpec((1, count, tokens), spots(order)) for _, _, count, order in layout]

    def accumulate(total, terms, decay):
        block = pl.BlockSpec((pairs * pair_rows, col_count), lambda i, place: (i, 0))
        whole = pl.BlockSpec((tokens, col_count), lambda i, place: (0, 0))
        arrays = [array for rows, _, x in terms for array in (*rows, x)]
        shape = jax.ShapeDtypeStruct((row_count, col_count), jnp.float32)
        layouts = [[piece and piece[:3] for piece in layout] for _, layout, _ in terms]
        return pl.pallas_call(
            functools.partial(accumulate_kernel, layouts, decay),
            grid_spec=pltpu.PrefetchScalarGridSpec(
                num_scalar_prefetch=1,
                grid=(owners // pairs,),
                in_specs=[block] + [spec for _, layout, _ in terms for spec in (*term_specs(layout), whole)],
                out_specs=block,
            ),
            out_shape=shape,
            compiler_params=pltpu.CompilerParams(vmem_limit_bytes=VMEM_BYTES),
            cost_estimate=pl.CostEstimate(
                flops=2 * len(terms) * tokens * row_count * col_count,
                bytes_accessed=2 * row_count * (len(terms) * tokens + 4 * col_count),
                transcendentals=0,
            ),
        )(place, total, *arrays)

    whole_pair = [[(core, 0, pair_rows, order) for core in range(2)] for order in range(2)]
    halves = [(core, part * half, half, part) for part in range(2) for core in range(2)]
    own = ([query_grads], [None], inputs)
    one = ([near[0], near_got[0]], whole_pair[0], moved_1)
    two = ([far[0], far_got[0], far[1], far_got[1]], halves, moved_2)
    total = accumulate(momentum, [own, one], MOMENTUM_DECAY)
    total = accumulate(total, [two], None)

    whole_vmem = pl.BlockSpec(memory_space=pltpu.VMEM)
    anywhere = pl.BlockSpec(memory_space=pl.ANY)
    in_smem = pl.BlockSpec(memory_space=pltpu.SMEM)
    count = owners // 2
    whole_shape = jax.ShapeDtypeStruct((row_count, col_count), jnp.float32)
    block_shape = jax.ShapeDtypeStruct((count, pair_rows, col_count), jnp.float32)

    sems = pltpu.SemaphoreType.DMA((2, count))
    params = pltpu.CompilerParams(vmem_limit_bytes=VMEM_BYTES)

    def last(core, rows):
        return pl.pallas_call(
            functools.partial(last_kernel, core),
            in_specs=[in_smem] + [whole_vmem] * 3,
            out_specs=[whole_vmem, whole_vmem],
            out_shape=[
                block_shape,
                jax.ShapeDtypeStruct((count, pair_heads, HEAD_DIM, HEAD_DIM), jnp.float32),
            ],
            compiler_params=params,
            cost_estimate=pl.CostEstimate(
                flops=tokens * row_count * col_count, bytes_accessed=2 * row_count * col_count, transcendentals=0
            ),
        )(place, total, rows, moved_3)

    other_blocks, gram = last(1, near_got[1])
    arrived = over(1, gram)
    own_blocks, gram = last(0, near[1])
    new_momentum = pl.pallas_call(
        store_kernel,
        in_specs=[in_smem] + [whole_vmem] * 2,
        out_specs=anywhere,
        out_shape=whole_shape,
        scratch_shapes=[sems],
        compiler_params=params,
        cost_estimate=pl.CostEstimate(flops=0, bytes_accessed=8 * row_count * col_count, transcendentals=0),
    )(place, own_blocks, other_blocks)
    four = gram + arrived
    pieces = [four[0]] + [over(2 * i, four[i]) for i in range(1, 4)]
    pieces, new_momentum = lax.optimization_barrier((pieces, new_momentum))
    factor = pl.pallas_call(
        polynomial_kernel,
        out_shape=jax.ShapeDtypeStruct(pieces[0].shape, jnp.float32),
        compiler_params=pltpu.CompilerParams(vmem_limit_bytes=SMALL_BYTES),
    )(*pieces)
    factors = jnp.stack([factor] + [over(2 * i, factor) for i in range(1, 4)])
    others = over(1, factors)

    scale = math.sqrt(model_width)
    cost = pl.CostEstimate(
        flops=3 * row_count * col_count * HEAD_DIM, bytes_accessed=2 * row_count * col_count, transcendentals=0
    )
    held = pl.pallas_call(
        functools.partial(own_update_kernel, scale),
        in_specs=[whole_vmem] * 2,
        out_specs=whole_vmem,
        out_shape=block_shape,
        compiler_params=params,
        cost_estimate=cost,
    )(factors, own_blocks)
    update = pl.pallas_call(
        functools.partial(other_update_kernel, scale),
        in_specs=[in_smem] + [whole_vmem] * 3,
        out_specs=anywhere,
        out_shape=whole_shape,
        scratch_shapes=[pltpu.VMEM(block_shape.shape, jnp.float32), sems],
        compiler_params=params,
        cost_estimate=cost,
    )(place, others, other_blocks, held)
    return new_momentum, update


def polynomial(gram_matrix):
    matrix_order = gram_matrix.shape[-1]
    trace_sum = jnp.sum(jnp.diagonal(gram_matrix, axis1=1, axis2=2), axis=1)
    norm_scale = jnp.sqrt(trace_sum) + NORM_EPS
    current = gram_matrix / (norm_scale * norm_scale)[:, None, None]
    identity = jnp.eye(matrix_order, dtype=jnp.float32)
    factor = jnp.broadcast_to(identity, gram_matrix.shape)
    for sweep_index in range(NEWTON_STEPS):
        square = jnp.einsum("hij,hjk->hik", current, current, precision=HIGHEST)
        poly_term = LINEAR_COEF * identity + CUBIC_COEF * current + QUINTIC_COEF * square
        factor = jnp.einsum("hij,hjk->hik", poly_term, factor, precision=HIGHEST)
        if sweep_index + 1 < NEWTON_STEPS:
            inner = jnp.einsum("hij,hjk->hik", current, poly_term, precision=HIGHEST)
            current = jnp.einsum("hij,hjk->hik", poly_term, inner, precision=HIGHEST)
    return factor / norm_scale[:, None, None]


def plain_shards(model_width, inputs, query_grads, momentum):
    row_count, col_count = momentum.shape
    gradient = lax.psum_scatter(
        lax.dot_general(query_grads, inputs, CONTRACT_TOKENS, preferred_element_type=jnp.float32),
        "dp",
        scatter_dimension=0,
        tiled=True,
    )
    new_momentum = MOMENTUM_DECAY * momentum + gradient
    local_heads = row_count // HEAD_DIM
    blocks = new_momentum.reshape(local_heads, HEAD_DIM, col_count)
    partial_value = jnp.einsum("hik,hjk->hij", blocks, blocks, precision=HIGHEST)
    owners = lax.axis_size("cols")
    slot_count = -(-local_heads // owners)
    padded = jnp.pad(partial_value, ((0, slot_count * owners - local_heads), (0, 0), (0, 0)))
    owned_gram = lax.psum_scatter(
        padded.reshape(slot_count, owners, HEAD_DIM, HEAD_DIM), "cols", scatter_dimension=1, tiled=True
    )
    owned_factor = polynomial(owned_gram.reshape(slot_count, HEAD_DIM, HEAD_DIM))
    returned = lax.all_gather(
        owned_factor.reshape(slot_count, 1, HEAD_DIM, HEAD_DIM), "cols", axis=1, tiled=True
    )
    factor = returned.reshape(slot_count * owners, HEAD_DIM, HEAD_DIM)[:local_heads]
    update = math.sqrt(model_width) * jnp.einsum("hij,hjk->hik", factor, blocks, precision=HIGHEST)
    return new_momentum, update.reshape(row_count, col_count)


def solution(mesh):
    depth, owners = mesh.shape["dp"], mesh.shape["cols"]

    def run(inputs, query_grads, momentum):
        local_heads = momentum.shape[0] // depth // HEAD_DIM
        chosen = shards if (depth, owners) == (4, 8) and local_heads % owners == 0 else plain_shards
        return jax.shard_map(
            functools.partial(chosen, momentum.shape[1]),
            mesh=mesh,
            in_specs=(P("dp", "cols"), P("dp", None), P("dp", "cols")),
            out_specs=(P("dp", "cols"), P("dp", "cols")),
            check_vma=False,
        )(inputs, query_grads, momentum)

    return run
```

```python
import functools
import math

import jax
import jax.numpy as jnp
from jax import lax
from jax.experimental import pallas as pl
from jax.experimental.pallas import tpu as pltpu
from jax.sharding import PartitionSpec as P

HEAD_DIM = 128
NEWTON_STEPS = 5
MOMENTUM_DECAY = 0.95
NORM_EPS = 1e-07
LINEAR_COEF = 3.4445
CUBIC_COEF = -4.775
QUINTIC_COEF = 2.0315
HIGHEST = lax.Precision.HIGHEST
CONTRACT_TOKENS = (((0,), (0,)), ((), ()))
SMALL_BYTES = 16 * 1024 * 1024
VMEM_BYTES = 32 * 1024 * 1024


def split(value):
    high = value.astype(jnp.bfloat16)
    return high, (value - high.astype(jnp.float32)).astype(jnp.bfloat16)


def dot3(left, right):
    dot = functools.partial(jnp.dot, preferred_element_type=jnp.float32)
    both = dot(jnp.concatenate(left), right[0])
    rows = left[0].shape[0]
    return both[:rows] + (both[rows:] + dot(left[0], right[1]))


def gram_of(block):
    high, low = split(block)
    both = lax.dot_general(
        jnp.concatenate([high, low]), high, (((1,), (1,)), ((), ())), preferred_element_type=jnp.float32
    )
    rows = high.shape[0]
    cross = both[rows:]
    return both[:rows] + (cross + cross.T)


def accumulate_kernel(layouts, decay, place, total, *refs):
    refs, out = list(refs[:-1]), refs[-1]
    out[...] = total[...] * decay if decay else total[...]
    pair_rows = out.shape[0] // 2
    for layout in layouts:
        q_refs, x_ref = [refs.pop(0) for _ in layout], refs.pop(0)
        for q_ref, piece in zip(q_refs, layout):
            if piece is None:
                out[...] += lax.dot_general(
                    q_ref[...], x_ref[...], CONTRACT_TOKENS, preferred_element_type=jnp.float32
                )
                continue
            core, offset, count = piece
            start = pl.multiple_of(((place[1] + core) % 2) * pair_rows + offset, count)
            value = jnp.dot(q_ref[0], x_ref[...], preferred_element_type=jnp.float32)
            out[pl.ds(start, count), :] += value


def rows_at(place, core, index, count):
    return pl.ds(pl.multiple_of((place[1] ^ (2 * index + core)) * count, count), count)


def last_kernel(core, place, total, queries, x_ref, blocks, gram):
    count = queries.shape[1]
    depth = queries.shape[2]
    product = jnp.dot(queries[...].reshape(-1, depth), x_ref[...], preferred_element_type=jnp.float32)
    for index in range(queries.shape[0]):
        value = total[rows_at(place, core, index, count), :] + product[index * count : (index + 1) * count, :]
        blocks[index] = value
        for head in range(gram.shape[1]):
            gram[index, head] = gram_of(value[head * HEAD_DIM : (head + 1) * HEAD_DIM, :])


def store_kernel(place, own, other, out, sems):
    copies = []
    for core, blocks in enumerate((own, other)):
        for index in range(blocks.shape[0]):
            rows = rows_at(place, core, index, blocks.shape[1])
            copies.append(pltpu.make_async_copy(blocks.at[index], out.at[rows, :], sems.at[core, index]))
            copies[-1].start()
    for copy in copies:
        copy.wait()


def polynomial_kernel(*refs):
    parts, factor = refs[:-1], refs[-1]
    gram = functools.reduce(lambda total, piece: total + piece[...], parts[1:], parts[0][...])
    order = gram.shape[-1]
    rows = lax.broadcasted_iota(jnp.int32, (order, order), 0)
    cols = lax.broadcasted_iota(jnp.int32, (order, order), 1)
    identity = (rows == cols).astype(jnp.float32)
    heads = range(gram.shape[0])

    dot = functools.partial(jnp.dot, precision=HIGHEST, preferred_element_type=jnp.float32)
    norms = [jnp.sqrt(jnp.sum(gram[h] * identity)) + NORM_EPS for h in heads]
    current = [gram[h] / (norms[h] * norms[h]) for h in heads]
    factors = [None for h in heads]
    for sweep in range(NEWTON_STEPS):
        square = [dot(current[h], current[h]) for h in heads]
        poly = [LINEAR_COEF * identity + CUBIC_COEF * current[h] + QUINTIC_COEF * square[h] for h in heads]
        factors = [poly[h] if sweep == 0 else dot(poly[h], factors[h]) for h in heads]
        if sweep + 1 < NEWTON_STEPS:
            inner = [dot(current[h], poly[h]) for h in heads]
            current = [dot(poly[h], inner[h]) for h in heads]
    for h in heads:
        factor[h] = factors[h] / norms[h]


def updated(scale, factor, block):
    heads = []
    for head in range(factor.shape[0]):
        rows = slice(head * HEAD_DIM, (head + 1) * HEAD_DIM)
        heads.append(scale * dot3(split(factor[head]), split(block[rows, :])))
    return jnp.concatenate(heads)


def own_update_kernel(scale, factor, blocks, held):
    for index in range(blocks.shape[0]):
        held[index] = updated(scale, factor[index], blocks[index])


def other_update_kernel(scale, place, factor, blocks, own, update, held, sems):
    def send(core, source, index):
        rows = rows_at(place, core, index, blocks.shape[1])
        copy = pltpu.make_async_copy(source.at[index], update.at[rows, :], sems.at[core, index])
        copy.start()
        return copy

    copies = [send(0, own, index) for index in range(own.shape[0])]
    for index in range(blocks.shape[0]):
        held[index] = updated(scale, factor[index], blocks[index])
        copies.append(send(1, held, index))
    for copy in copies:
        copy.wait()


def shards(model_width, inputs, query_grads, momentum):
    depth = lax.axis_size("dp")
    owners = lax.axis_size("cols")
    z = lax.axis_index("dp")
    c = lax.axis_index("cols")
    tokens, col_count = inputs.shape
    row_count = momentum.shape[0]
    pair_rows = row_count // owners
    pair_heads = pair_rows // HEAD_DIM
    def over(bits, value):
        return lax.ppermute(value, "cols", [(i, i ^ bits) for i in range(owners)])

    def onward(k, value):
        return lax.ppermute(value, "dp", [(i, (i + k) % depth) for i in range(depth)])

    def over_halves(bits, value):
        axis = 0 if value.shape[0] > 1 else 1
        return jnp.concatenate([over(bits, piece) for piece in jnp.split(value, 2, axis)], axis)

    def both(held, got):
        return [jnp.concatenate(pair) for pair in zip(held, got)]

    pieces = [
        lax.dynamic_slice(query_grads, (0, lax.rem(z + k, depth) * row_count + c * pair_rows), (tokens, pair_rows)).T
        for k in range(1, depth)
    ]
    turns = ((4, 2), (2, 4))
    half = pair_rows // 2

    near = [onward(k, pieces[k - 1]) for k in (1, 3)]
    near = lax.optimization_barrier(near)

    far = onward(2, pieces[1])
    near = [piece[None] for piece in near]
    got = [over_halves(turn[0], piece) for turn, piece in zip(turns, near)]
    far, near, got, moved = lax.optimization_barrier((far, near, got, inputs))

    moved_1 = onward(1, moved)
    near = both(near, got)
    got = [over_halves(turn[1], piece) for turn, piece in zip(turns, near)]
    far, near, got, moved_1 = lax.optimization_barrier((far, near, got, moved_1))

    moved_2 = onward(1, moved_1)
    near = both(near, got)
    near_got = [over(1, piece) for piece in near]
    far = [far[None, :half], far[None, half:]]
    far = both(far, [over(turn[0], piece) for turn, piece in zip(turns, far)])
    got = [over(turn[1], piece) for turn, piece in zip(turns, far)]
    far, near, near_got, got, moved_1, moved_2 = lax.optimization_barrier((far, near, near_got, got, moved_1, moved_2))

    moved_3 = onward(1, moved_2)
    far = both(far, got)
    far_got = [over(1, piece) for piece in far]

    place = jnp.stack([z, c]).astype(jnp.int32)

    def pair_of(i, place):
        return place[1] ^ ((i % 4) * 2 + i // 4)

    def rows_spec(part, columns):
        return pl.BlockSpec((pair_rows, columns), lambda i, place: (pair_of(i, place), part))

    pairs = 2
    def spots(order):
        def index_map(i, place):
            other = (place[1] // 2) ^ i
            return (other if order else (other % 2) * 2 + other // 2), 0, 0

        return index_map

    def term_specs(layout):
        if layout[0] is None:
            return [pl.BlockSpec((tokens, pairs * pair_rows), lambda i, place: (0, place[0] * (owners // pairs) + i))]
        return [pl.BlockSpec((1, count, tokens), spots(order)) for _, _, count, order in layout]

    def accumulate(total, terms, decay):
        block = pl.BlockSpec((pairs * pair_rows, col_count), lambda i, place: (i, 0))
        whole = pl.BlockSpec((tokens, col_count), lambda i, place: (0, 0))
        arrays = [array for rows, _, x in terms for array in (*rows, x)]
        shape = jax.ShapeDtypeStruct((row_count, col_count), jnp.float32)
        layouts = [[piece and piece[:3] for piece in layout] for _, layout, _ in terms]
        return pl.pallas_call(
            functools.partial(accumulate_kernel, layouts, decay),
            grid_spec=pltpu.PrefetchScalarGridSpec(
                num_scalar_prefetch=1,
                grid=(owners // pairs,),
                in_specs=[block] + [spec for _, layout, _ in terms for spec in (*term_specs(layout), whole)],
                out_specs=block,
            ),
            out_shape=shape,
            compiler_params=pltpu.CompilerParams(vmem_limit_bytes=VMEM_BYTES),
            cost_estimate=pl.CostEstimate(
                flops=2 * len(terms) * tokens * row_count * col_count,
                bytes_accessed=2 * row_count * (len(terms) * tokens + 4 * col_count),
                transcendentals=0,
            ),
        )(place, total, *arrays)

    whole_pair = [[(core, 0, pair_rows, order) for core in range(2)] for order in range(2)]
    halves = [(core, part * half, half, part) for part in range(2) for core in range(2)]
    own = ([query_grads], [None], inputs)
    one = ([near[0], near_got[0]], whole_pair[0], moved_1)
    two = ([far[0], far_got[0], far[1], far_got[1]], halves, moved_2)
    total = accumulate(momentum, [own, one], MOMENTUM_DECAY)
    total = accumulate(total, [two], None)

    whole_vmem = pl.BlockSpec(memory_space=pltpu.VMEM)
    anywhere = pl.BlockSpec(memory_space=pl.ANY)
    in_smem = pl.BlockSpec(memory_space=pltpu.SMEM)
    count = owners // 2
    whole_shape = jax.ShapeDtypeStruct((row_count, col_count), jnp.float32)
    block_shape = jax.ShapeDtypeStruct((count, pair_rows, col_count), jnp.float32)

    sems = pltpu.SemaphoreType.DMA((2, count))
    params = pltpu.CompilerParams(vmem_limit_bytes=VMEM_BYTES)

    def last(core, rows):
        return pl.pallas_call(
            functools.partial(last_kernel, core),
            in_specs=[in_smem] + [whole_vmem] * 3,
            out_specs=[whole_vmem, whole_vmem],
            out_shape=[
                block_shape,
                jax.ShapeDtypeStruct((count, pair_heads, HEAD_DIM, HEAD_DIM), jnp.float32),
            ],
            compiler_params=params,
            cost_estimate=pl.CostEstimate(
                flops=tokens * row_count * col_count, bytes_accessed=2 * row_count * col_count, transcendentals=0
            ),
        )(place, total, rows, moved_3)

    other_blocks, gram = last(1, near_got[1])
    arrived = over(1, gram)
    own_blocks, gram = last(0, near[1])
    new_momentum = pl.pallas_call(
        store_kernel,
        in_specs=[in_smem] + [whole_vmem] * 2,
        out_specs=anywhere,
        out_shape=whole_shape,
        scratch_shapes=[sems],
        compiler_params=params,
        cost_estimate=pl.CostEstimate(flops=0, bytes_accessed=8 * row_count * col_count, transcendentals=0),
    )(place, own_blocks, other_blocks)
    four = gram + arrived
    pieces = [four[0]] + [over(2 * i, four[i]) for i in range(1, 4)]
    pieces, new_momentum = lax.optimization_barrier((pieces, new_momentum))
    factor = pl.pallas_call(
        polynomial_kernel,
        out_shape=jax.ShapeDtypeStruct(pieces[0].shape, jnp.float32),
        compiler_params=pltpu.CompilerParams(vmem_limit_bytes=SMALL_BYTES),
    )(*pieces)
    factors = jnp.stack([factor] + [over(2 * i, factor) for i in range(1, 4)])
    others = over(1, factors)

    scale = math.sqrt(model_width)
    cost = pl.CostEstimate(
        flops=3 * row_count * col_count * HEAD_DIM, bytes_accessed=2 * row_count * col_count, transcendentals=0
    )
    held = pl.pallas_call(
        functools.partial(own_update_kernel, scale),
        in_specs=[whole_vmem] * 2,
        out_specs=whole_vmem,
        out_shape=block_shape,
        compiler_params=params,
        cost_estimate=cost,
    )(factors, own_blocks)
    update = pl.pallas_call(
        functools.partial(other_update_kernel, scale),
        in_specs=[in_smem] + [whole_vmem] * 3,
        out_specs=anywhere,
        out_shape=whole_shape,
        scratch_shapes=[pltpu.VMEM(block_shape.shape, jnp.float32), sems],
        compiler_params=params,
        cost_estimate=cost,
    )(place, others, other_blocks, held)
    return new_momentum, update


def polynomial(gram_matrix):
    matrix_order = gram_matrix.shape[-1]
    trace_sum = jnp.sum(jnp.diagonal(gram_matrix, axis1=1, axis2=2), axis=1)
    norm_scale = jnp.sqrt(trace_sum) + NORM_EPS
    current = gram_matrix / (norm_scale * norm_scale)[:, None, None]
    identity = jnp.eye(matrix_order, dtype=jnp.float32)
    factor = jnp.broadcast_to(identity, gram_matrix.shape)
    for sweep_index in range(NEWTON_STEPS):
        square = jnp.einsum("hij,hjk->hik", current, current, precision=HIGHEST)
        poly_term = LINEAR_COEF * identity + CUBIC_COEF * current + QUINTIC_COEF * square
        factor = jnp.einsum("hij,hjk->hik", poly_term, factor, precision=HIGHEST)
        if sweep_index + 1 < NEWTON_STEPS:
            inner = jnp.einsum("hij,hjk->hik", current, poly_term, precision=HIGHEST)
            current = jnp.einsum("hij,hjk->hik", poly_term, inner, precision=HIGHEST)
    return factor / norm_scale[:, None, None]


def plain_shards(model_width, inputs, query_grads, momentum):
    row_count, col_count = momentum.shape
    gradient = lax.psum_scatter(
        lax.dot_general(query_grads, inputs, CONTRACT_TOKENS, preferred_element_type=jnp.float32),
        "dp",
        scatter_dimension=0,
        tiled=True,
    )
    new_momentum = MOMENTUM_DECAY * momentum + gradient
    local_heads = row_count // HEAD_DIM
    blocks = new_momentum.reshape(local_heads, HEAD_DIM, col_count)
    partial_value = jnp.einsum("hik,hjk->hij", blocks, blocks, precision=HIGHEST)
    owners = lax.axis_size("cols")
    slot_count = -(-local_heads // owners)
    padded = jnp.pad(partial_value, ((0, slot_count * owners - local_heads), (0, 0), (0, 0)))
    owned_gram = lax.psum_scatter(
        padded.reshape(slot_count, owners, HEAD_DIM, HEAD_DIM), "cols", scatter_dimension=1, tiled=True
    )
    owned_factor = polynomial(owned_gram.reshape(slot_count, HEAD_DIM, HEAD_DIM))
    returned = lax.all_gather(
        owned_factor.reshape(slot_count, 1, HEAD_DIM, HEAD_DIM), "cols", axis=1, tiled=True
    )
    factor = returned.reshape(slot_count * owners, HEAD_DIM, HEAD_DIM)[:local_heads]
    update = math.sqrt(model_width) * jnp.einsum("hij,hjk->hik", factor, blocks, precision=HIGHEST)
    return new_momentum, update.reshape(row_count, col_count)


def solution(mesh):
    depth, owners = mesh.shape["dp"], mesh.shape["cols"]

    def run(inputs, query_grads, momentum):
        local_heads = momentum.shape[0] // depth // HEAD_DIM
        chosen = shards if (depth, owners) == (4, 8) and local_heads % owners == 0 else plain_shards
        return jax.shard_map(
            functools.partial(chosen, momentum.shape[1]),
            mesh=mesh,
            in_specs=(P("dp", "cols"), P("dp", None), P("dp", "cols")),
            out_specs=(P("dp", "cols"), P("dp", "cols")),
            check_vma=False,
        )(inputs, query_grads, momentum)

    return run
```

```python
import functools
import math

import jax
import jax.numpy as jnp
from jax import lax
from jax.experimental import pallas as pl
from jax.experimental.pallas import tpu as pltpu
from jax.sharding import PartitionSpec as P

HEAD_DIM = 128
NEWTON_STEPS = 5
MOMENTUM_DECAY = 0.95
NORM_EPS = 1e-07
LINEAR_COEF = 3.4445
CUBIC_COEF = -4.775
QUINTIC_COEF = 2.0315
HIGHEST = lax.Precision.HIGHEST
CONTRACT_TOKENS = (((0,), (0,)), ((), ()))
SMALL_BYTES = 16 * 1024 * 1024
VMEM_BYTES = 32 * 1024 * 1024


def split(value):
    high = value.astype(jnp.bfloat16)
    return high, (value - high.astype(jnp.float32)).astype(jnp.bfloat16)


def dot3(left, right):
    dot = functools.partial(jnp.dot, preferred_element_type=jnp.float32)
    both = dot(jnp.concatenate(left), right[0])
    rows = left[0].shape[0]
    return both[:rows] + (both[rows:] + dot(left[0], right[1]))


def gram_of(block):
    high, low = split(block)
    both = lax.dot_general(
        jnp.concatenate([high, low]), high, (((1,), (1,)), ((), ())), preferred_element_type=jnp.float32
    )
    rows = high.shape[0]
    cross = both[rows:]
    return both[:rows] + (cross + cross.T)


def accumulate_kernel(layouts, decay, place, total, *refs):
    refs, out = list(refs[:-1]), refs[-1]
    out[...] = total[...] * decay if decay else total[...]
    pair_rows = out.shape[0] // 2
    for layout in layouts:
        q_refs, x_ref = [refs.pop(0) for _ in layout], refs.pop(0)
        for q_ref, piece in zip(q_refs, layout):
            if piece is None:
                out[...] += lax.dot_general(
                    q_ref[...], x_ref[...], CONTRACT_TOKENS, preferred_element_type=jnp.float32
                )
                continue
            core, offset, count = piece
            start = pl.multiple_of(((place[1] + core) % 2) * pair_rows + offset, count)
            value = jnp.dot(q_ref[0], x_ref[...], preferred_element_type=jnp.float32)
            out[pl.ds(start, count), :] += value


def rows_at(place, core, index, count):
    return pl.ds(pl.multiple_of((place[1] ^ (2 * index + core)) * count, count), count)


def last_kernel(core, place, total, queries, x_ref, blocks, gram):
    count = queries.shape[1]
    depth = queries.shape[2]
    product = jnp.dot(queries[...].reshape(-1, depth), x_ref[...], preferred_element_type=jnp.float32)
    for index in range(queries.shape[0]):
        value = total[rows_at(place, core, index, count), :] + product[index * count : (index + 1) * count, :]
        blocks[index] = value
        for head in range(gram.shape[1]):
            gram[index, head] = gram_of(value[head * HEAD_DIM : (head + 1) * HEAD_DIM, :])


def store_kernel(place, own, other, out, sems):
    copies = []
    for core, blocks in enumerate((own, other)):
        for index in range(blocks.shape[0]):
            rows = rows_at(place, core, index, blocks.shape[1])
            copies.append(pltpu.make_async_copy(blocks.at[index], out.at[rows, :], sems.at[core, index]))
            copies[-1].start()
    for copy in copies:
        copy.wait()


def polynomial_kernel(*refs):
    parts, factor = refs[:-1], refs[-1]
    gram = functools.reduce(lambda total, piece: total + piece[...], parts[1:], parts[0][...])
    order = gram.shape[-1]
    rows = lax.broadcasted_iota(jnp.int32, (order, order), 0)
    cols = lax.broadcasted_iota(jnp.int32, (order, order), 1)
    identity = (rows == cols).astype(jnp.float32)
    heads = range(gram.shape[0])

    dot = functools.partial(jnp.dot, precision=HIGHEST, preferred_element_type=jnp.float32)
    norms = [jnp.sqrt(jnp.sum(gram[h] * identity)) + NORM_EPS for h in heads]
    current = [gram[h] / (norms[h] * norms[h]) for h in heads]
    factors = [None for h in heads]
    for sweep in range(NEWTON_STEPS):
        square = [dot(current[h], current[h]) for h in heads]
        poly = [LINEAR_COEF * identity + CUBIC_COEF * current[h] + QUINTIC_COEF * square[h] for h in heads]
        factors = [poly[h] if sweep == 0 else dot(poly[h], factors[h]) for h in heads]
        if sweep + 1 < NEWTON_STEPS:
            inner = [dot(current[h], poly[h]) for h in heads]
            current = [dot(poly[h], inner[h]) for h in heads]
    for h in heads:
        factor[h] = factors[h] / norms[h]


def updated(scale, factor, block):
    heads = []
    for head in range(factor.shape[0]):
        rows = slice(head * HEAD_DIM, (head + 1) * HEAD_DIM)
        heads.append(scale * dot3(split(factor[head]), split(block[rows, :])))
    return jnp.concatenate(heads)


def own_update_kernel(scale, factor, blocks, held):
    for index in range(blocks.shape[0]):
        held[index] = updated(scale, factor[index], blocks[index])


def other_update_kernel(scale, place, factor, blocks, own, update, held, sems):
    def send(core, source, index):
        rows = rows_at(place, core, index, blocks.shape[1])
        copy = pltpu.make_async_copy(source.at[index], update.at[rows, :], sems.at[core, index])
        copy.start()
        return copy

    copies = [send(0, own, index) for index in range(own.shape[0])]
    for index in range(blocks.shape[0]):
        held[index] = updated(scale, factor[index], blocks[index])
        copies.append(send(1, held, index))
    for copy in copies:
        copy.wait()


def shards(model_width, inputs, query_grads, momentum):
    depth = lax.axis_size("dp")
    owners = lax.axis_size("cols")
    z = lax.axis_index("dp")
    c = lax.axis_index("cols")
    tokens, col_count = inputs.shape
    row_count = momentum.shape[0]
    pair_rows = row_count // owners
    pair_heads = pair_rows // HEAD_DIM
    def over(bits, value):
        return lax.ppermute(value, "cols", [(i, i ^ bits) for i in range(owners)])

    def onward(k, value):
        return lax.ppermute(value, "dp", [(i, (i + k) % depth) for i in range(depth)])

    def over_halves(bits, value):
        axis = 0 if value.shape[0] > 1 else 1
        return jnp.concatenate([over(bits, piece) for piece in jnp.split(value, 2, axis)], axis)

    def both(held, got):
        return [jnp.concatenate(pair) for pair in zip(held, got)]

    taken, starts = {}, [lax.rem(z + k, depth) * row_count + c * pair_rows for k in range(depth)]
    for k in (1, 3, 2):
        taken[k] = lax.dynamic_slice(query_grads, (0, starts[k]), (tokens, pair_rows)).T
        taken[k], starts = lax.optimization_barrier((taken[k], starts))
    pieces = [taken[k] for k in range(1, depth)]
    turns = ((4, 2), (2, 4))
    half = pair_rows // 2

    near = [onward(k, pieces[k - 1]) for k in (1, 3)]
    near = lax.optimization_barrier(near)

    far = onward(2, pieces[1])
    near = [piece[None] for piece in near]
    got = [over_halves(turn[0], piece) for turn, piece in zip(turns, near)]
    far, near, got, moved = lax.optimization_barrier((far, near, got, inputs))

    moved_1 = onward(1, moved)
    near = both(near, got)
    got = [over_halves(turn[1], piece) for turn, piece in zip(turns, near)]
    far, near, got, moved_1 = lax.optimization_barrier((far, near, got, moved_1))

    moved_2 = onward(1, moved_1)
    near = both(near, got)
    near_got = [over(1, piece) for piece in near]
    far = [far[None, :half], far[None, half:]]
    far = both(far, [over(turn[0], piece) for turn, piece in zip(turns, far)])
    got = [over(turn[1], piece) for turn, piece in zip(turns, far)]
    far, near, near_got, got, moved_1, moved_2 = lax.optimization_barrier((far, near, near_got, got, moved_1, moved_2))

    moved_3 = onward(1, moved_2)
    far = both(far, got)
    far_got = [over(1, piece) for piece in far]

    place = jnp.stack([z, c]).astype(jnp.int32)

    def pair_of(i, place):
        return place[1] ^ ((i % 4) * 2 + i // 4)

    def rows_spec(part, columns):
        return pl.BlockSpec((pair_rows, columns), lambda i, place: (pair_of(i, place), part))

    pairs = 2
    def spots(order):
        def index_map(i, place):
            other = (place[1] // 2) ^ i
            return (other if order else (other % 2) * 2 + other // 2), 0, 0

        return index_map

    def term_specs(layout):
        if layout[0] is None:
            return [pl.BlockSpec((tokens, pairs * pair_rows), lambda i, place: (0, place[0] * (owners // pairs) + i))]
        return [pl.BlockSpec((1, count, tokens), spots(order)) for _, _, count, order in layout]

    def accumulate(total, terms, decay):
        block = pl.BlockSpec((pairs * pair_rows, col_count), lambda i, place: (i, 0))
        whole = pl.BlockSpec((tokens, col_count), lambda i, place: (0, 0))
        arrays = [array for rows, _, x in terms for array in (*rows, x)]
        shape = jax.ShapeDtypeStruct((row_count, col_count), jnp.float32)
        layouts = [[piece and piece[:3] for piece in layout] for _, layout, _ in terms]
        return pl.pallas_call(
            functools.partial(accumulate_kernel, layouts, decay),
            grid_spec=pltpu.PrefetchScalarGridSpec(
                num_scalar_prefetch=1,
                grid=(owners // pairs,),
                in_specs=[block] + [spec for _, layout, _ in terms for spec in (*term_specs(layout), whole)],
                out_specs=block,
            ),
            out_shape=shape,
            compiler_params=pltpu.CompilerParams(vmem_limit_bytes=VMEM_BYTES),
            cost_estimate=pl.CostEstimate(
                flops=2 * len(terms) * tokens * row_count * col_count,
                bytes_accessed=2 * row_count * (len(terms) * tokens + 4 * col_count),
                transcendentals=0,
            ),
        )(place, total, *arrays)

    whole_pair = [[(core, 0, pair_rows, order) for core in range(2)] for order in range(2)]
    halves = [(core, part * half, half, part) for part in range(2) for core in range(2)]
    own = ([query_grads], [None], inputs)
    one = ([near[0], near_got[0]], whole_pair[0], moved_1)
    two = ([far[0], far_got[0], far[1], far_got[1]], halves, moved_2)
    total = accumulate(momentum, [own, one], MOMENTUM_DECAY)
    total = accumulate(total, [two], None)

    whole_vmem = pl.BlockSpec(memory_space=pltpu.VMEM)
    anywhere = pl.BlockSpec(memory_space=pl.ANY)
    in_smem = pl.BlockSpec(memory_space=pltpu.SMEM)
    count = owners // 2
    whole_shape = jax.ShapeDtypeStruct((row_count, col_count), jnp.float32)
    block_shape = jax.ShapeDtypeStruct((count, pair_rows, col_count), jnp.float32)

    sems = pltpu.SemaphoreType.DMA((2, count))
    params = pltpu.CompilerParams(vmem_limit_bytes=VMEM_BYTES)

    def last(core, rows):
        return pl.pallas_call(
            functools.partial(last_kernel, core),
            in_specs=[in_smem] + [whole_vmem] * 3,
            out_specs=[whole_vmem, whole_vmem],
            out_shape=[
                block_shape,
                jax.ShapeDtypeStruct((count, pair_heads, HEAD_DIM, HEAD_DIM), jnp.float32),
            ],
            compiler_params=params,
            cost_estimate=pl.CostEstimate(
                flops=tokens * row_count * col_count, bytes_accessed=2 * row_count * col_count, transcendentals=0
            ),
        )(place, total, rows, moved_3)

    other_blocks, gram = last(1, near_got[1])
    arrived = over(1, gram)
    own_blocks, gram = last(0, near[1])
    new_momentum = pl.pallas_call(
        store_kernel,
        in_specs=[in_smem] + [whole_vmem] * 2,
        out_specs=anywhere,
        out_shape=whole_shape,
        scratch_shapes=[sems],
        compiler_params=params,
        cost_estimate=pl.CostEstimate(flops=0, bytes_accessed=8 * row_count * col_count, transcendentals=0),
    )(place, own_blocks, other_blocks)
    four = gram + arrived
    pieces = [four[0]] + [over(2 * i, four[i]) for i in range(1, 4)]
    pieces, new_momentum = lax.optimization_barrier((pieces, new_momentum))
    factor = pl.pallas_call(
        polynomial_kernel,
        out_shape=jax.ShapeDtypeStruct(pieces[0].shape, jnp.float32),
        compiler_params=pltpu.CompilerParams(vmem_limit_bytes=SMALL_BYTES),
    )(*pieces)
    factors = jnp.stack([factor] + [over(2 * i, factor) for i in range(1, 4)])
    others = over(1, factors)

    scale = math.sqrt(model_width)
    cost = pl.CostEstimate(
        flops=3 * row_count * col_count * HEAD_DIM, bytes_accessed=2 * row_count * col_count, transcendentals=0
    )
    held = pl.pallas_call(
        functools.partial(own_update_kernel, scale),
        in_specs=[whole_vmem] * 2,
        out_specs=whole_vmem,
        out_shape=block_shape,
        compiler_params=params,
        cost_estimate=cost,
    )(factors, own_blocks)
    update = pl.pallas_call(
        functools.partial(other_update_kernel, scale),
        in_specs=[in_smem] + [whole_vmem] * 3,
        out_specs=anywhere,
        out_shape=whole_shape,
        scratch_shapes=[pltpu.VMEM(block_shape.shape, jnp.float32), sems],
        compiler_params=params,
        cost_estimate=cost,
    )(place, others, other_blocks, held)
    return new_momentum, update


def polynomial(gram_matrix):
    matrix_order = gram_matrix.shape[-1]
    trace_sum = jnp.sum(jnp.diagonal(gram_matrix, axis1=1, axis2=2), axis=1)
    norm_scale = jnp.sqrt(trace_sum) + NORM_EPS
    current = gram_matrix / (norm_scale * norm_scale)[:, None, None]
    identity = jnp.eye(matrix_order, dtype=jnp.float32)
    factor = jnp.broadcast_to(identity, gram_matrix.shape)
    for sweep_index in range(NEWTON_STEPS):
        square = jnp.einsum("hij,hjk->hik", current, current, precision=HIGHEST)
        poly_term = LINEAR_COEF * identity + CUBIC_COEF * current + QUINTIC_COEF * square
        factor = jnp.einsum("hij,hjk->hik", poly_term, factor, precision=HIGHEST)
        if sweep_index + 1 < NEWTON_STEPS:
            inner = jnp.einsum("hij,hjk->hik", current, poly_term, precision=HIGHEST)
            current = jnp.einsum("hij,hjk->hik", poly_term, inner, precision=HIGHEST)
    return factor / norm_scale[:, None, None]


def plain_shards(model_width, inputs, query_grads, momentum):
    row_count, col_count = momentum.shape
    gradient = lax.psum_scatter(
        lax.dot_general(query_grads, inputs, CONTRACT_TOKENS, preferred_element_type=jnp.float32),
        "dp",
        scatter_dimension=0,
        tiled=True,
    )
    new_momentum = MOMENTUM_DECAY * momentum + gradient
    local_heads = row_count // HEAD_DIM
    blocks = new_momentum.reshape(local_heads, HEAD_DIM, col_count)
    partial_value = jnp.einsum("hik,hjk->hij", blocks, blocks, precision=HIGHEST)
    owners = lax.axis_size("cols")
    slot_count = -(-local_heads // owners)
    padded = jnp.pad(partial_value, ((0, slot_count * owners - local_heads), (0, 0), (0, 0)))
    owned_gram = lax.psum_scatter(
        padded.reshape(slot_count, owners, HEAD_DIM, HEAD_DIM), "cols", scatter_dimension=1, tiled=True
    )
    owned_factor = polynomial(owned_gram.reshape(slot_count, HEAD_DIM, HEAD_DIM))
    returned = lax.all_gather(
        owned_factor.reshape(slot_count, 1, HEAD_DIM, HEAD_DIM), "cols", axis=1, tiled=True
    )
    factor = returned.reshape(slot_count * owners, HEAD_DIM, HEAD_DIM)[:local_heads]
    update = math.sqrt(model_width) * jnp.einsum("hij,hjk->hik", factor, blocks, precision=HIGHEST)
    return new_momentum, update.reshape(row_count, col_count)


def solution(mesh):
    depth, owners = mesh.shape["dp"], mesh.shape["cols"]

    def run(inputs, query_grads, momentum):
        local_heads = momentum.shape[0] // depth // HEAD_DIM
        chosen = shards if (depth, owners) == (4, 8) and local_heads % owners == 0 else plain_shards
        return jax.shard_map(
            functools.partial(chosen, momentum.shape[1]),
            mesh=mesh,
            in_specs=(P("dp", "cols"), P("dp", None), P("dp", "cols")),
            out_specs=(P("dp", "cols"), P("dp", "cols")),
            check_vma=False,
        )(inputs, query_grads, momentum)

    return run
```

```python
import functools
import math

import jax
import jax.numpy as jnp
from jax import lax
from jax.experimental import pallas as pl
from jax.experimental.pallas import tpu as pltpu
from jax.sharding import PartitionSpec as P

HEAD_DIM = 128
NEWTON_STEPS = 5
MOMENTUM_DECAY = 0.95
NORM_EPS = 1e-07
LINEAR_COEF = 3.4445
CUBIC_COEF = -4.775
QUINTIC_COEF = 2.0315
HIGHEST = lax.Precision.HIGHEST
CONTRACT_TOKENS = (((0,), (0,)), ((), ()))
SMALL_BYTES = 16 * 1024 * 1024
VMEM_BYTES = 32 * 1024 * 1024


def split(value):
    high = value.astype(jnp.bfloat16)
    return high, (value - high.astype(jnp.float32)).astype(jnp.bfloat16)


def dot3(left, right):
    dot = functools.partial(jnp.dot, preferred_element_type=jnp.float32)
    both = dot(jnp.concatenate(left), right[0])
    rows = left[0].shape[0]
    return both[:rows] + (both[rows:] + dot(left[0], right[1]))


def gram_of(block):
    high, low = split(block)
    both = lax.dot_general(
        jnp.concatenate([high, low]), high, (((1,), (1,)), ((), ())), preferred_element_type=jnp.float32
    )
    rows = high.shape[0]
    cross = both[rows:]
    return both[:rows] + (cross + cross.T)


def accumulate_kernel(layouts, decay, place, total, *refs):
    refs, out = list(refs[:-1]), refs[-1]
    out[...] = total[...] * decay if decay else total[...]
    pair_rows = out.shape[0] // 2
    for layout in layouts:
        q_refs, x_ref = [refs.pop(0) for _ in layout], refs.pop(0)
        for q_ref, piece in zip(q_refs, layout):
            if piece is None:
                out[...] += lax.dot_general(
                    q_ref[...], x_ref[...], CONTRACT_TOKENS, preferred_element_type=jnp.float32
                )
                continue
            core, offset, count = piece
            start = pl.multiple_of(((place[1] + core) % 2) * pair_rows + offset, count)
            value = jnp.dot(q_ref[0], x_ref[...], preferred_element_type=jnp.float32)
            out[pl.ds(start, count), :] += value


def rows_at(place, core, index, count):
    return pl.ds(pl.multiple_of((place[1] ^ (2 * index + core)) * count, count), count)


def last_kernel(core, place, total, queries, x_ref, blocks, gram):
    count = queries.shape[1]
    depth = queries.shape[2]
    product = jnp.dot(queries[...].reshape(-1, depth), x_ref[...], preferred_element_type=jnp.float32)
    for index in range(queries.shape[0]):
        value = total[rows_at(place, core, index, count), :] + product[index * count : (index + 1) * count, :]
        blocks[index] = value
        for head in range(gram.shape[1]):
            gram[index, head] = gram_of(value[head * HEAD_DIM : (head + 1) * HEAD_DIM, :])


def store_kernel(place, own, other, out, sems):
    copies = []
    for core, blocks in enumerate((own, other)):
        for index in range(blocks.shape[0]):
            rows = rows_at(place, core, index, blocks.shape[1])
            copies.append(pltpu.make_async_copy(blocks.at[index], out.at[rows, :], sems.at[core, index]))
            copies[-1].start()
    for copy in copies:
        copy.wait()


def polynomial_kernel(*refs):
    parts, factor = refs[:-1], refs[-1]
    gram = functools.reduce(lambda total, piece: total + piece[...], parts[1:], parts[0][...])
    order = gram.shape[-1]
    rows = lax.broadcasted_iota(jnp.int32, (order, order), 0)
    cols = lax.broadcasted_iota(jnp.int32, (order, order), 1)
    identity = (rows == cols).astype(jnp.float32)
    heads = range(gram.shape[0])

    dot = functools.partial(jnp.dot, precision=HIGHEST, preferred_element_type=jnp.float32)
    norms = [jnp.sqrt(jnp.sum(gram[h] * identity)) + NORM_EPS for h in heads]
    current = [gram[h] / (norms[h] * norms[h]) for h in heads]
    factors = [None for h in heads]
    for sweep in range(NEWTON_STEPS):
        square = [dot(current[h], current[h]) for h in heads]
        poly = [LINEAR_COEF * identity + CUBIC_COEF * current[h] + QUINTIC_COEF * square[h] for h in heads]
        factors = [poly[h] if sweep == 0 else dot(poly[h], factors[h]) for h in heads]
        if sweep + 1 < NEWTON_STEPS:
            inner = [dot(current[h], poly[h]) for h in heads]
            current = [dot(poly[h], inner[h]) for h in heads]
    for h in heads:
        factor[h] = factors[h] / norms[h]


def updated(scale, factor, block):
    heads = []
    for head in range(factor.shape[0]):
        rows = slice(head * HEAD_DIM, (head + 1) * HEAD_DIM)
        heads.append(scale * dot3(split(factor[head]), split(block[rows, :])))
    return jnp.concatenate(heads)


def own_update_kernel(scale, factor, blocks, held):
    for index in range(blocks.shape[0]):
        held[index] = updated(scale, factor[index], blocks[index])


def other_update_kernel(scale, place, factor, blocks, own, update, held, sems):
    def send(core, source, index):
        rows = rows_at(place, core, index, blocks.shape[1])
        copy = pltpu.make_async_copy(source.at[index], update.at[rows, :], sems.at[core, index])
        copy.start()
        return copy

    copies = [send(0, own, index) for index in range(own.shape[0])]
    for index in range(blocks.shape[0]):
        held[index] = updated(scale, factor[index], blocks[index])
        copies.append(send(1, held, index))
    for copy in copies:
        copy.wait()


def shards(model_width, inputs, query_grads, momentum):
    depth = lax.axis_size("dp")
    owners = lax.axis_size("cols")
    z = lax.axis_index("dp")
    c = lax.axis_index("cols")
    tokens, col_count = inputs.shape
    row_count = momentum.shape[0]
    pair_rows = row_count // owners
    pair_heads = pair_rows // HEAD_DIM
    def over(bits, value):
        return lax.ppermute(value, "cols", [(i, i ^ bits) for i in range(owners)])

    def onward(k, value):
        return lax.ppermute(value, "dp", [(i, (i + k) % depth) for i in range(depth)])

    def over_halves(bits, value):
        axis = 0 if value.shape[0] > 1 else 1
        return jnp.concatenate([over(bits, piece) for piece in jnp.split(value, 2, axis)], axis)

    def both(held, got):
        return [jnp.concatenate(pair) for pair in zip(held, got)]

    starts = [lax.rem(z + k, depth) * row_count + c * pair_rows for k in range(depth)]

    def taken(start):
        return lax.dynamic_slice(query_grads, (0, start), (tokens, pair_rows)).T

    first, third, starts = lax.optimization_barrier((taken(starts[1]), taken(starts[3]), starts))
    pieces = [first, taken(starts[2]), third]
    turns = ((4, 2), (2, 4))
    half = pair_rows // 2

    near = [onward(k, pieces[k - 1]) for k in (1, 3)]
    near = lax.optimization_barrier(near)

    far = onward(2, pieces[1])
    near = [piece[None] for piece in near]
    got = [over_halves(turn[0], piece) for turn, piece in zip(turns, near)]
    far, near, got, moved = lax.optimization_barrier((far, near, got, inputs))

    moved_1 = onward(1, moved)
    near = both(near, got)
    got = [over_halves(turn[1], piece) for turn, piece in zip(turns, near)]
    far, near, got, moved_1 = lax.optimization_barrier((far, near, got, moved_1))

    moved_2 = onward(1, moved_1)
    near = both(near, got)
    near_got = [over(1, piece) for piece in near]
    far = [far[None, :half], far[None, half:]]
    far = both(far, [over(turn[0], piece) for turn, piece in zip(turns, far)])
    got = [over(turn[1], piece) for turn, piece in zip(turns, far)]
    far, near, near_got, got, moved_1, moved_2 = lax.optimization_barrier((far, near, near_got, got, moved_1, moved_2))

    moved_3 = onward(1, moved_2)
    far = both(far, got)
    far_got = [over(1, piece) for piece in far]

    place = jnp.stack([z, c]).astype(jnp.int32)

    def pair_of(i, place):
        return place[1] ^ ((i % 4) * 2 + i // 4)

    def rows_spec(part, columns):
        return pl.BlockSpec((pair_rows, columns), lambda i, place: (pair_of(i, place), part))

    pairs = 2
    def spots(order):
        def index_map(i, place):
            other = (place[1] // 2) ^ i
            return (other if order else (other % 2) * 2 + other // 2), 0, 0

        return index_map

    def term_specs(layout):
        if layout[0] is None:
            return [pl.BlockSpec((tokens, pairs * pair_rows), lambda i, place: (0, place[0] * (owners // pairs) + i))]
        return [pl.BlockSpec((1, count, tokens), spots(order)) for _, _, count, order in layout]

    def accumulate(total, terms, decay):
        block = pl.BlockSpec((pairs * pair_rows, col_count), lambda i, place: (i, 0))
        whole = pl.BlockSpec((tokens, col_count), lambda i, place: (0, 0))
        arrays = [array for rows, _, x in terms for array in (*rows, x)]
        shape = jax.ShapeDtypeStruct((row_count, col_count), jnp.float32)
        layouts = [[piece and piece[:3] for piece in layout] for _, layout, _ in terms]
        return pl.pallas_call(
            functools.partial(accumulate_kernel, layouts, decay),
            grid_spec=pltpu.PrefetchScalarGridSpec(
                num_scalar_prefetch=1,
                grid=(owners // pairs,),
                in_specs=[block] + [spec for _, layout, _ in terms for spec in (*term_specs(layout), whole)],
                out_specs=block,
            ),
            out_shape=shape,
            compiler_params=pltpu.CompilerParams(vmem_limit_bytes=VMEM_BYTES),
            cost_estimate=pl.CostEstimate(
                flops=2 * len(terms) * tokens * row_count * col_count,
                bytes_accessed=2 * row_count * (len(terms) * tokens + 4 * col_count),
                transcendentals=0,
            ),
        )(place, total, *arrays)

    whole_pair = [[(core, 0, pair_rows, order) for core in range(2)] for order in range(2)]
    halves = [(core, part * half, half, part) for part in range(2) for core in range(2)]
    own = ([query_grads], [None], inputs)
    one = ([near[0], near_got[0]], whole_pair[0], moved_1)
    two = ([far[0], far_got[0], far[1], far_got[1]], halves, moved_2)
    total = accumulate(momentum, [own, one], MOMENTUM_DECAY)
    total = accumulate(total, [two], None)

    whole_vmem = pl.BlockSpec(memory_space=pltpu.VMEM)
    anywhere = pl.BlockSpec(memory_space=pl.ANY)
    in_smem = pl.BlockSpec(memory_space=pltpu.SMEM)
    count = owners // 2
    whole_shape = jax.ShapeDtypeStruct((row_count, col_count), jnp.float32)
    block_shape = jax.ShapeDtypeStruct((count, pair_rows, col_count), jnp.float32)

    sems = pltpu.SemaphoreType.DMA((2, count))
    params = pltpu.CompilerParams(vmem_limit_bytes=VMEM_BYTES)

    def last(core, rows):
        return pl.pallas_call(
            functools.partial(last_kernel, core),
            in_specs=[in_smem] + [whole_vmem] * 3,
            out_specs=[whole_vmem, whole_vmem],
            out_shape=[
                block_shape,
                jax.ShapeDtypeStruct((count, pair_heads, HEAD_DIM, HEAD_DIM), jnp.float32),
            ],
            compiler_params=params,
            cost_estimate=pl.CostEstimate(
                flops=tokens * row_count * col_count, bytes_accessed=2 * row_count * col_count, transcendentals=0
            ),
        )(place, total, rows, moved_3)

    other_blocks, gram = last(1, near_got[1])
    arrived = over(1, gram)
    own_blocks, gram = last(0, near[1])
    new_momentum = pl.pallas_call(
        store_kernel,
        in_specs=[in_smem] + [whole_vmem] * 2,
        out_specs=anywhere,
        out_shape=whole_shape,
        scratch_shapes=[sems],
        compiler_params=params,
        cost_estimate=pl.CostEstimate(flops=0, bytes_accessed=8 * row_count * col_count, transcendentals=0),
    )(place, own_blocks, other_blocks)
    four = gram + arrived
    pieces = [four[0]] + [over(2 * i, four[i]) for i in range(1, 4)]
    pieces, new_momentum = lax.optimization_barrier((pieces, new_momentum))
    factor = pl.pallas_call(
        polynomial_kernel,
        out_shape=jax.ShapeDtypeStruct(pieces[0].shape, jnp.float32),
        compiler_params=pltpu.CompilerParams(vmem_limit_bytes=SMALL_BYTES),
    )(*pieces)
    factors = jnp.stack([factor] + [over(2 * i, factor) for i in range(1, 4)])
    others = over(1, factors)

    scale = math.sqrt(model_width)
    cost = pl.CostEstimate(
        flops=3 * row_count * col_count * HEAD_DIM, bytes_accessed=2 * row_count * col_count, transcendentals=0
    )
    held = pl.pallas_call(
        functools.partial(own_update_kernel, scale),
        in_specs=[whole_vmem] * 2,
        out_specs=whole_vmem,
        out_shape=block_shape,
        compiler_params=params,
        cost_estimate=cost,
    )(factors, own_blocks)
    update = pl.pallas_call(
        functools.partial(other_update_kernel, scale),
        in_specs=[in_smem] + [whole_vmem] * 3,
        out_specs=anywhere,
        out_shape=whole_shape,
        scratch_shapes=[pltpu.VMEM(block_shape.shape, jnp.float32), sems],
        compiler_params=params,
        cost_estimate=cost,
    )(place, others, other_blocks, held)
    return new_momentum, update


def polynomial(gram_matrix):
    matrix_order = gram_matrix.shape[-1]
    trace_sum = jnp.sum(jnp.diagonal(gram_matrix, axis1=1, axis2=2), axis=1)
    norm_scale = jnp.sqrt(trace_sum) + NORM_EPS
    current = gram_matrix / (norm_scale * norm_scale)[:, None, None]
    identity = jnp.eye(matrix_order, dtype=jnp.float32)
    factor = jnp.broadcast_to(identity, gram_matrix.shape)
    for sweep_index in range(NEWTON_STEPS):
        square = jnp.einsum("hij,hjk->hik", current, current, precision=HIGHEST)
        poly_term = LINEAR_COEF * identity + CUBIC_COEF * current + QUINTIC_COEF * square
        factor = jnp.einsum("hij,hjk->hik", poly_term, factor, precision=HIGHEST)
        if sweep_index + 1 < NEWTON_STEPS:
            inner = jnp.einsum("hij,hjk->hik", current, poly_term, precision=HIGHEST)
            current = jnp.einsum("hij,hjk->hik", poly_term, inner, precision=HIGHEST)
    return factor / norm_scale[:, None, None]


def plain_shards(model_width, inputs, query_grads, momentum):
    row_count, col_count = momentum.shape
    gradient = lax.psum_scatter(
        lax.dot_general(query_grads, inputs, CONTRACT_TOKENS, preferred_element_type=jnp.float32),
        "dp",
        scatter_dimension=0,
        tiled=True,
    )
    new_momentum = MOMENTUM_DECAY * momentum + gradient
    local_heads = row_count // HEAD_DIM
    blocks = new_momentum.reshape(local_heads, HEAD_DIM, col_count)
    partial_value = jnp.einsum("hik,hjk->hij", blocks, blocks, precision=HIGHEST)
    owners = lax.axis_size("cols")
    slot_count = -(-local_heads // owners)
    padded = jnp.pad(partial_value, ((0, slot_count * owners - local_heads), (0, 0), (0, 0)))
    owned_gram = lax.psum_scatter(
        padded.reshape(slot_count, owners, HEAD_DIM, HEAD_DIM), "cols", scatter_dimension=1, tiled=True
    )
    owned_factor = polynomial(owned_gram.reshape(slot_count, HEAD_DIM, HEAD_DIM))
    returned = lax.all_gather(
        owned_factor.reshape(slot_count, 1, HEAD_DIM, HEAD_DIM), "cols", axis=1, tiled=True
    )
    factor = returned.reshape(slot_count * owners, HEAD_DIM, HEAD_DIM)[:local_heads]
    update = math.sqrt(model_width) * jnp.einsum("hij,hjk->hik", factor, blocks, precision=HIGHEST)
    return new_momentum, update.reshape(row_count, col_count)


def solution(mesh):
    depth, owners = mesh.shape["dp"], mesh.shape["cols"]

    def run(inputs, query_grads, momentum):
        local_heads = momentum.shape[0] // depth // HEAD_DIM
        chosen = shards if (depth, owners) == (4, 8) and local_heads % owners == 0 else plain_shards
        return jax.shard_map(
            functools.partial(chosen, momentum.shape[1]),
            mesh=mesh,
            in_specs=(P("dp", "cols"), P("dp", None), P("dp", "cols")),
            out_specs=(P("dp", "cols"), P("dp", "cols")),
            check_vma=False,
        )(inputs, query_grads, momentum)

    return run
```
